32 devices in a mesh: dp: 8 (over z, y), tensor: 4 (over x, core).
Axes of the slice: x: 2, y: 2, z: 4, core: 2. Of those that a mesh axis runs over, the one named last changes fastest.
Arguments:
- layer_input: bfloat16 [2048, 2048], P('dp'), may hold values from -6 to 6
- upstream: bfloat16 [2048, 2048], P('dp'), may hold values from -6 to 6
- norm_gains: float32 [4, 2048], replicated, may hold values from 0.5 to 1.5
- mixer_input: bfloat16 [2048, 2, 4096], P('dp', None, 'tensor'), may hold values from -0.125 to 0.125
- conv_taps: float32 [4, 4096], P(None, 'tensor'), may hold values from -3 to 3
- conv_bias: float32 [4096], P('tensor'), may hold values from -1.8 to 1.8
- mixer_select: bfloat16 [160, 4096], P('dp', 'tensor'), may hold values from -0.09375 to 0.09375
- mixer_step: bfloat16 [128, 4096], P('dp', 'tensor'), may hold values from -0.5 to 0.5
- step_bias: float32 [4096], P('tensor'), may hold values from -6.5 to -2.5
- decay_log: float32 [16, 4096], P(None, 'tensor'), may hold values from 0 to 2.77
- skip_gain: float32 [4096], P('tensor'), may hold values from 0.1 to 1.9
- mixer_output: bfloat16 [2048, 4096], P('dp', 'tensor'), may hold values from -0.09375 to 0.09375
- first_gate_up: bfloat16 [2048, 2, 4096], P('dp', None, 'tensor'), may hold values from -0.125 to 0.125
- first_down: bfloat16 [2048, 4096], P('dp', 'tensor'), may hold values from -0.09375 to 0.09375
- attention_input: bfloat16 [2048, 3, 2048], P('dp', None, 'tensor'), may hold values from -0.125 to 0.125
- attention_output: bfloat16 [2048, 2048], P('dp', 'tensor'), may hold values from -1.5 to 1.5
- second_gate_up: bfloat16 [2048, 2, 4096], P('dp', None, 'tensor'), may hold values from -0.125 to 0.125
- second_down: bfloat16 [2048, 4096], P('dp', 'tensor'), may hold values from -0.09375 to 0.09375
Outputs:
- layer_output: bfloat16 [2048, 2048], P('dp')
- input_gradient: float32 [2048, 2048], P('dp')
- norm_gains_gradient: float32 [4, 2048], replicated
- mixer_input_gradient: float32 [2048, 2, 4096], P('dp', None, 'tensor')
- conv_taps_gradient: float32 [4, 4096], P(None, 'tensor')
- conv_bias_gradient: float32 [4096], P('tensor')
- mixer_select_gradient: float32 [160, 4096], P('dp', 'tensor')
- mixer_step_gradient: float32 [128, 4096], P('dp', 'tensor')
- step_bias_gradient: float32 [4096], P('tensor')
- decay_log_gradient: float32 [16, 4096], P(None, 'tensor')
- skip_gain_gradient: float32 [4096], P('tensor')
- mixer_output_gradient: float32 [2048, 4096], P('dp', 'tensor')
- first_gate_up_gradient: float32 [2048, 2, 4096], P('dp', None, 'tensor')
- first_down_gradient: float32 [2048, 4096], P('dp', 'tensor')
- attention_input_gradient: float32 [2048, 3, 2048], P('dp', None, 'tensor')
- attention_output_gradient: float32 [2048, 2048], P('dp', 'tensor')
- second_gate_up_gradient: float32 [2048, 2, 4096], P('dp', None, 'tensor')
- second_down_gradient: float32 [2048, 4096], P('dp', 'tensor')
The draws below stay inside these ranges and needn't reach their ends.
All inputs are finite; a program needn't handle non-finite values.
Results may differ from the reference program's by a relative error of at most 0.033.
Values may be sent and summed in bfloat16 or wider, within the bound.
No kernel may reach another device: no remote copies, remote signals or barrier semaphores. Data moves between devices by JAX's collectives and lax.ppermute only.
A program may use at most 256 MiB of HBM per device.

```python
import math
import jax
import jax.numpy as jnp
from jax import lax

D = 2048
INNER = 4096
STATE = 16
CONV = 4
DT_RANK = 128
FF = 4096
HEADS = 32
HEAD_DIM = 64
WINDOW = 2048
NORMS = 4
SEQ = 256
TOKENS = 2048
XDBL = 160
QDIM = 2048
N_DP = 8


def shard_levels(rng, extent, cuts, smallest, high):
    def one(position, blocks):
        draws = jax.random.uniform(jax.random.fold_in(jax.random.fold_in(rng, 6), position), (blocks,), jnp.float32, smallest / len(cuts), high / len(cuts))
        return jnp.repeat(jnp.exp(draws), extent[position] // blocks).reshape((-1,) + (1,) * (len(extent) - position - 1))

    loudness = one(*cuts[0])
    for cut in cuts[1:]:
        loudness = loudness * one(*cut)
    return loudness


def gaussian(own_key, dims, deviation, bound, shards=(), held_as=jnp.bfloat16):
    entries = deviation * jax.random.normal(own_key, dims, jnp.float32)
    if shards:
        entries = entries * shard_levels(own_key, dims, shards, -0.22, 0.18)
    return jnp.clip(entries, -bound, bound).astype(held_as)


def setup_inputs(seed: int = 0) -> dict:
    key_of = jax.random.split(jax.random.key(seed), 19)
    return {
        "layer_input": gaussian(key_of[0], (TOKENS, D), 1.0, 6.0, ((0, 8),)),
        "upstream": gaussian(key_of[1], (TOKENS, D), 1.0, 6.0, ((0, 8),)),
        "norm_gains": jnp.clip(1.0 + 0.1 * jax.random.normal(key_of[2], (NORMS, D), jnp.float32), 0.5, 1.5),
        "mixer_input": gaussian(key_of[3], (D, 2, INNER), D ** -0.5, 0.125, ((0, 8), (2, 4))),
        "conv_taps": gaussian(key_of[4], (CONV, INNER), 0.5, 3.0, ((1, 4),), jnp.float32),
        "conv_bias": gaussian(key_of[5], (INNER,), 0.3, 1.8, ((0, 4),), jnp.float32),
        "mixer_select": gaussian(key_of[6], (XDBL, INNER), INNER ** -0.5, 0.09375, ((0, 8), (1, 4))),
        "mixer_step": gaussian(key_of[7], (DT_RANK, INNER), DT_RANK ** -0.5, 0.5, ((0, 8), (1, 4))),
        "step_bias": jnp.clip(-6.5 + 4.0 * jax.random.uniform(key_of[8], (INNER,), jnp.float32) ** shard_levels(key_of[8], (INNER,), ((0, 4),), -0.2, 0.2), -6.5, -2.5),
        "decay_log": jnp.clip(2.77 * jax.random.uniform(key_of[9], (STATE, INNER), jnp.float32) ** shard_levels(key_of[9], (STATE, INNER), ((1, 4),), -0.2, 0.2), 0.0, 2.77),
        "skip_gain": jnp.clip(1.0 + 0.18 * jax.random.normal(key_of[10], (INNER,), jnp.float32), 0.1, 1.9),
        "mixer_output": gaussian(key_of[11], (D, INNER), INNER ** -0.5, 0.09375, ((0, 8), (1, 4))),
        "first_gate_up": gaussian(key_of[12], (D, 2, FF), D ** -0.5, 0.125, ((0, 8), (2, 4))),
        "first_down": gaussian(key_of[13], (D, FF), FF ** -0.5, 0.09375, ((0, 8), (1, 4))),
        "attention_input": gaussian(key_of[14], (D, 3, QDIM), D ** -0.5, 0.125, ((0, 8), (2, 4))),
        "attention_output": gaussian(key_of[15], (D, QDIM), (max(HEADS * HEAD_DIM // 128, 2)) ** -0.5, 1.5, ((0, 8), (1, 4))),
        "second_gate_up": gaussian(key_of[16], (D, 2, FF), D ** -0.5, 0.125, ((0, 8), (2, 4))),
        "second_down": gaussian(key_of[17], (D, FF), FF ** -0.5, 0.09375, ((0, 8), (1, 4))),
    }


EPS = 1e-05
ROPE_BASE = 10000.0
MASKED = -1e+30
PRECISE = lax.Precision.HIGHEST

@jax.custom_vjp
def low(v):
    return lax.optimization_barrier(v.astype(jnp.bfloat16)).astype(jnp.float32)

@jax.custom_vjp
def low_back(v):
    return v

def low_keep(v):
    return (low(v), None)

def low_pass(kept, grad):
    return (grad,)

def back_keep(v):
    return (v, None)

def back_low(kept, grad):
    return (low(grad),)
low.defvjp(low_keep, low_pass)
low_back.defvjp(back_keep, back_low)

def rms_scaled(stream, gain_row):
    return stream * lax.rsqrt(lax.optimization_barrier(jnp.mean(stream * stream, axis=-1, keepdims=True)) + EPS) * gain_row[None, :]

def conv_silu(inner_in, conv_taps, conv_bias):
    length = inner_in.shape[0]
    kernel_size = conv_taps.shape[0]
    padded = jnp.pad(inner_in, ((kernel_size - 1, 0), (0, 0)))
    conv_total = conv_bias[None, :] + jnp.zeros_like(inner_in)
    for offset in range(kernel_size):
        conv_total = conv_total + conv_taps[offset][None, :] * padded[offset:offset + length]
    return jax.nn.silu(conv_total)

def gated_scan(conv_out, gate_val, step_raw, select_b, select_c, step_bias, decay_log, skip_gain):
    length, channels = conv_out.shape
    states_n = select_b.shape[1]
    step_size = jax.nn.softplus(step_raw + step_bias[None, :])
    decay_rate = -jnp.exp(decay_log)
    block_len = math.gcd(length, 64)
    block_count = length // block_len

    def combine(earlier, latter):
        return (earlier[0] * latter[0], latter[0] * earlier[1] + latter[1])

    def one_block(carry_state, pieces):
        seq_x, seq_step, seq_b, seq_c = pieces
        factor = jnp.exp(seq_step[:, None, :] * decay_rate[None, :, :])
        drive_term = (seq_step * seq_x)[:, None, :] * seq_b[:, :, None]
        cum_factor, cum_drive = lax.associative_scan(combine, (factor, drive_term), axis=0)
        states = cum_factor * carry_state[None] + cum_drive
        result = lax.optimization_barrier(jnp.sum(seq_c[:, :, None] * states, axis=1))
        return (states[-1], result)
    pieces = (conv_out.reshape(block_count, block_len, channels), step_size.reshape(block_count, block_len, channels), select_b.reshape(block_count, block_len, states_n), select_c.reshape(block_count, block_len, states_n))
    zero_state = jnp.zeros((states_n, channels), jnp.float32)
    last_state, outputs = lax.scan(jax.checkpoint(one_block), zero_state, pieces)
    mixed = outputs.reshape(length, channels) + skip_gain[None, :] * conv_out
    return mixed * jax.nn.silu(gate_val)

def rotate(values, direction):
    length, heads_n, size_head = values.shape
    half_size = size_head // 2
    positions = jnp.arange(length, dtype=jnp.float32)
    frequency = ROPE_BASE ** (-jnp.arange(half_size, dtype=jnp.float32) * 2.0 / size_head)
    angles = positions[:, None] * frequency[None, :]
    cosine = jnp.cos(angles)[:, None, :]
    sine_part = direction * jnp.sin(angles)[:, None, :]
    first_half = values[..., :half_size]
    second_half = values[..., half_size:]
    return jnp.concatenate([first_half * cosine - second_half * sine_part, second_half * cosine + first_half * sine_part], axis=-1)

def window_mask(length):
    rows_at = jnp.arange(length)[:, None]
    cols_at = jnp.arange(length)[None, :]
    return (cols_at <= rows_at) & (rows_at - cols_at < WINDOW)

def mixer_block(stream, gain_row, mixer_input, conv_taps, conv_bias, mixer_select, mixer_step, step_bias, decay_log, skip_gain, mixer_output):
    normed = low(rms_scaled(stream, gain_row))
    paired = jnp.einsum('td,dkc->tkc', normed, mixer_input, precision=PRECISE)
    inner_in = low_back(paired[:, 0])
    gate_val = low_back(paired[:, 1])
    conv_out = low(conv_silu(inner_in, conv_taps, conv_bias))
    selected = low_back(jnp.einsum('tc,sc->ts', conv_out, mixer_select, precision=PRECISE))
    step_rank = mixer_step.shape[0]
    states_n = decay_log.shape[0]
    step_low = low(selected[:, :step_rank])
    select_b = selected[:, step_rank:step_rank + states_n]
    select_c = selected[:, step_rank + states_n:]
    step_raw = low_back(jnp.dot(step_low, mixer_step, precision=PRECISE))
    gated = low(gated_scan(conv_out, gate_val, step_raw, select_b, select_c, step_bias, decay_log, skip_gain))
    branch = low_back(jnp.einsum('tc,dc->td', gated, mixer_output, precision=PRECISE))
    return stream + branch

def feed_forward(stream, gain_row, gate_up, down_proj):
    normed = low(rms_scaled(stream, gain_row))
    paired = jnp.einsum('td,dkf->tkf', normed, gate_up, precision=PRECISE)
    gate_val = low_back(paired[:, 0])
    up_val = low_back(paired[:, 1])
    hidden = low(jax.nn.silu(gate_val) * up_val)
    branch = low_back(jnp.einsum('tf,df->td', hidden, down_proj, precision=PRECISE))
    return stream + branch

def attention_block(stream, gain_row, attention_input, attention_output):
    length = stream.shape[0]
    normed = low(rms_scaled(stream, gain_row))
    triple = jnp.einsum('td,dkq->tkq', normed, attention_input, precision=PRECISE)
    heads_n = triple.shape[2] // HEAD_DIM
    query_raw = low_back(triple[:, 0]).reshape(length, heads_n, HEAD_DIM)
    key_raw = low_back(triple[:, 1]).reshape(length, heads_n, HEAD_DIM)
    values = low(low_back(triple[:, 2])).reshape(length, heads_n, HEAD_DIM)
    queries = low(rotate(query_raw, 1.0))
    keys_rot = low(rotate(key_raw, 1.0))
    scores = low_back(jnp.einsum('qhd,khd->hqk', queries, keys_rot, precision=PRECISE) * HEAD_DIM ** (-0.5))
    scores = jnp.where(window_mask(length)[None], scores, MASKED)
    row_peak = lax.optimization_barrier(jnp.max(scores, axis=-1, keepdims=True))
    expanded = jnp.exp(scores - row_peak)
    attend = low(expanded / lax.optimization_barrier(jnp.sum(expanded, axis=-1, keepdims=True)))
    context = jnp.einsum('hqk,khd->qhd', attend, values, precision=PRECISE).reshape(length, heads_n * HEAD_DIM)
    context = low(low_back(context))
    branch = low_back(jnp.einsum('tq,dq->td', context, attention_output, precision=PRECISE))
    return stream + branch

def layer_forward(stream, params):
    norm_gains, mixer_input, conv_taps, conv_bias, mixer_select, mixer_step, step_bias, decay_log, skip_gain, mixer_output, first_gate_up, first_down, attention_input, attention_output, second_gate_up, second_down = params
    after_mixer = mixer_block(stream, norm_gains[0], mixer_input, conv_taps, conv_bias, mixer_select, mixer_step, step_bias, decay_log, skip_gain, mixer_output)
    after_first = feed_forward(after_mixer, norm_gains[1], first_gate_up, first_down)
    after_attention = attention_block(after_first, norm_gains[2], attention_input, attention_output)
    return feed_forward(after_attention, norm_gains[3], second_gate_up, second_down)

def reference(layer_input, upstream, norm_gains, mixer_input, conv_taps, conv_bias, mixer_select, mixer_step, step_bias, decay_log, skip_gain, mixer_output, first_gate_up, first_down, attention_input, attention_output, second_gate_up, second_down):
    params = tuple((member.astype(jnp.float32) for member in (norm_gains, mixer_input, conv_taps, conv_bias, mixer_select, mixer_step, step_bias, decay_log, skip_gain, mixer_output, first_gate_up, first_down, attention_input, attention_output, second_gate_up, second_down)))
    stream_all = layer_input.astype(jnp.float32).reshape(N_DP, SEQ, D)
    cotangent_all = upstream.astype(jnp.float32).reshape(N_DP, SEQ, D)

    def one_sequence(totals, couple):
        seq_rows, seq_cotangent = couple
        result, pull_back = jax.vjp(layer_forward, seq_rows, params)
        rows_grad, param_grads = pull_back(seq_cotangent)
        totals = jax.tree.map(lambda first_arg, second_arg: first_arg + second_arg, totals, param_grads)
        return (totals, (result.astype(jnp.bfloat16), rows_grad))
    zero_totals = jax.tree.map(jnp.zeros_like, params)
    totals, (outputs, rows_grads) = lax.scan(one_sequence, zero_totals, (stream_all, cotangent_all))
    return (outputs.reshape(TOKENS, D), rows_grads.reshape(TOKENS, D), totals[0], totals[1], totals[2], totals[3], totals[4], totals[5], totals[6], totals[7], totals[8], totals[9], totals[10], totals[11], totals[12], totals[13], totals[14], totals[15])
```

```python
import functools
import jax
import jax.numpy as jnp
from jax import lax
from jax.experimental import pallas as pl
from jax.experimental.pallas import tpu as pltpu
from jax.sharding import PartitionSpec as P

HEAD_DIM = 64
WINDOW = 2048
EPS = 1e-05
ROPE_BASE = 10000.0
MASKED = -1e30
BF = jnp.bfloat16
F32 = jnp.float32
SWAP = ((0, 1), (1, 0))
QUARTERS = 4
LANES = 128
ROWS = 8


def scan_forward_kernel(
    x_ref, raw_ref, gate_ref, sel_ref, bias_ref, decay_ref, skip_ref, y_ref, gated_ref, hist_ref, state_ref
):
    seqs, steps, channels = x_ref.shape
    blocks = channels // LANES
    states_n = decay_ref.shape[0]
    pairs = [(s, j) for s in range(seqs) for j in range(blocks)]

    @pl.when(pl.program_id(0) == 0)
    def _():
        state_ref[...] = jnp.zeros_like(state_ref)

    def lanes(j):
        return slice(j * LANES, (j + 1) * LANES)

    rates = [-jnp.exp(decay_ref[:, lanes(j)]) for j in range(blocks)]

    def chunk(k, states):
        states = list(states)
        rows = pl.ds(pl.multiple_of(k * ROWS, ROWS), ROWS)
        x_t, d_t, dx_t = {}, {}, {}
        for s, j in pairs:
            x_t[s, j] = x_ref[s, rows, lanes(j)]
            d_t[s, j] = jax.nn.softplus(raw_ref[s, rows, lanes(j)] + bias_ref[:, lanes(j)])
            dx_t[s, j] = d_t[s, j] * x_t[s, j]
        outs = {p: [] for p in pairs}
        for i in range(ROWS):
            for s in range(seqs):
                sel_b = jnp.broadcast_to(sel_ref[s, k, :states_n, i : i + 1], (states_n, LANES))
                sel_c = jnp.broadcast_to(sel_ref[s, k, states_n:, i : i + 1], (states_n, LANES))
                for j in range(blocks):
                    at = s * blocks + j
                    before = states[at]
                    hist_ref[s, k * ROWS + i, :, lanes(j)] = before
                    factor = jnp.exp(d_t[s, j][i : i + 1] * rates[j])
                    after = factor * before + dx_t[s, j][i : i + 1] * sel_b
                    states[at] = after
                    outs[s, j].append(jnp.sum(after * sel_c, axis=0, keepdims=True))
        for s, j in pairs:
            y = jnp.concatenate(outs[s, j], axis=0) + skip_ref[:, lanes(j)] * x_t[s, j]
            gate = gate_ref[s, rows, lanes(j)]
            y_ref[s, rows, lanes(j)] = y
            gated_ref[s, rows, lanes(j)] = y * gate * jax.nn.sigmoid(gate)
        return tuple(states)

    first = tuple(state_ref[s * blocks + j] for s, j in pairs)
    last = lax.fori_loop(0, steps // ROWS, chunk, first)
    for at, value in enumerate(last):
        state_ref[at] = value


def scan_backward_kernel(
    x_ref, raw_ref, gate_ref, y_ref, grad_ref, hist_ref, sel_ref, bias_ref, decay_ref, skip_ref,
    dgate_ref, dx_ref, draw_ref, dsel_ref, ddecay_ref, dskip_ref, dbias_ref, adj_ref,
):
    seqs, steps, channels = x_ref.shape
    blocks = channels // LANES
    states_n = decay_ref.shape[0]
    pairs = [(s, j) for s in range(seqs) for j in range(blocks)]

    @pl.when(pl.program_id(0) == 0)
    def _():
        adj_ref[...] = jnp.zeros_like(adj_ref)
        ddecay_ref[...] = jnp.zeros_like(ddecay_ref)
        dskip_ref[...] = jnp.zeros_like(dskip_ref)
        dbias_ref[...] = jnp.zeros_like(dbias_ref)

    def lanes(j):
        return slice(j * LANES, (j + 1) * LANES)

    rates = [-jnp.exp(decay_ref[:, lanes(j)]) for j in range(blocks)]
    columns = lax.broadcasted_iota(jnp.int32, (states_n, ROWS), 1)

    def chunk(step, carry):
        adjoint, decay_sum = list(carry[0]), list(carry[1])
        k = steps // ROWS - 1 - step
        rows = pl.ds(pl.multiple_of(k * ROWS, ROWS), ROWS)
        x_t, d_t, dx_t, dy_t, z_t = {}, {}, {}, {}, {}
        for s, j in pairs:
            x_t[s, j] = x_ref[s, rows, lanes(j)]
            z_t[s, j] = raw_ref[s, rows, lanes(j)] + bias_ref[:, lanes(j)]
            d_t[s, j] = jax.nn.softplus(z_t[s, j])
            dx_t[s, j] = d_t[s, j] * x_t[s, j]
            gate = gate_ref[s, rows, lanes(j)]
            sig = jax.nn.sigmoid(gate)
            grad = grad_ref[s, rows, lanes(j)]
            dy_t[s, j] = grad * gate * sig
            dgate_ref[s, rows, lanes(j)] = grad * y_ref[s, rows, lanes(j)] * sig * (1.0 + gate * (1.0 - sig))
        first, second = {p: [None] * ROWS for p in pairs}, {p: [None] * ROWS for p in pairs}
        for s in range(seqs):
            db_tile = jnp.zeros((states_n, ROWS), jnp.float32)
            dc_tile = jnp.zeros((states_n, ROWS), jnp.float32)
            for i in reversed(range(ROWS)):
                sel_b = jnp.broadcast_to(sel_ref[s, k, :states_n, i : i + 1], (states_n, LANES))
                sel_c = jnp.broadcast_to(sel_ref[s, k, states_n:, i : i + 1], (states_n, LANES))
                db = jnp.zeros((states_n, LANES), jnp.float32)
                dc = jnp.zeros((states_n, LANES), jnp.float32)
                for j in range(blocks):
                    at = s * blocks + j
                    before = hist_ref[s, k * ROWS + i, :, lanes(j)]
                    delta = d_t[s, j][i : i + 1]
                    drive = dx_t[s, j][i : i + 1]
                    dy = dy_t[s, j][i : i + 1]
                    factor = jnp.exp(delta * rates[j])
                    after = factor * before + drive * sel_b
                    lam = adjoint[at] + dy * sel_c
                    dc = dc + dy * after
                    db = db + drive * lam
                    first[s, j][i] = jnp.sum(lam * sel_b, axis=0, keepdims=True)
                    back = lam * factor
                    adjoint[at] = back
                    through = back * before
                    second[s, j][i] = jnp.sum(rates[j] * through, axis=0, keepdims=True)
                    decay_sum[at] = decay_sum[at] + delta * through
                db_tile = jnp.where(columns == i, jnp.sum(db, axis=1, keepdims=True), db_tile)
                dc_tile = jnp.where(columns == i, jnp.sum(dc, axis=1, keepdims=True), dc_tile)
            dsel_ref[s, k, :states_n, :] = db_tile
            dsel_ref[s, k, states_n:, :] = dc_tile
        for s, j in pairs:
            one = jnp.concatenate(first[s, j], axis=0)
            two = jnp.concatenate(second[s, j], axis=0)
            dx_ref[s, rows, lanes(j)] = dy_t[s, j] * skip_ref[:, lanes(j)] + d_t[s, j] * one
            draw = (two + x_t[s, j] * one) * jax.nn.sigmoid(z_t[s, j])
            draw_ref[s, rows, lanes(j)] = draw
            dskip_ref[:, lanes(j)] += dy_t[s, j] * x_t[s, j]
            dbias_ref[:, lanes(j)] += draw
        return tuple(adjoint), tuple(decay_sum)

    carry = (
        tuple(adj_ref[s * blocks + j] for s, j in pairs),
        tuple(jnp.zeros((states_n, LANES), jnp.float32) for _ in pairs),
    )
    adjoint, decay_sum = lax.fori_loop(0, steps // ROWS, chunk, carry)
    for at, value in enumerate(adjoint):
        adj_ref[at] = value
    for (s, j), value in zip(pairs, decay_sum):
        ddecay_ref[:, lanes(j)] += rates[j] * value


def chunk_steps(length):
    return 32 if length % 32 == 0 else length


def scan_forward(x, raw, gate, sel, bias, decay, skip):
    seqs, length, channels = x.shape
    states_n = decay.shape[0]
    steps = chunk_steps(length)
    act = pl.BlockSpec((seqs, steps, channels), lambda i: (0, i, 0))
    whole = lambda a: pl.BlockSpec(a.shape, lambda i: (0,) * a.ndim)
    vec = lambda v: v.reshape(1, -1)
    elems = seqs * length * channels * states_n
    return pl.pallas_call(
        scan_forward_kernel,
        grid=(length // steps,),
        in_specs=[act, act, act,
            pl.BlockSpec((seqs, steps // ROWS, 2 * states_n, ROWS), lambda i: (0, i, 0, 0)),
            whole(vec(bias)), whole(decay), whole(vec(skip))],
        out_specs=[act, act, pl.BlockSpec((seqs, steps, states_n, channels), lambda i: (0, i, 0, 0))],
        out_shape=[
            jax.ShapeDtypeStruct((seqs, length, channels), jnp.float32),
            jax.ShapeDtypeStruct((seqs, length, channels), jnp.float32),
            jax.ShapeDtypeStruct((seqs, length, states_n, channels), jnp.float32),
        ],
        scratch_shapes=[pltpu.VMEM((seqs * channels // LANES, states_n, LANES), jnp.float32)],
        cost_estimate=pl.CostEstimate(flops=8 * elems, bytes_accessed=4 * elems, transcendentals=elems),
        compiler_params=pltpu.CompilerParams(vmem_limit_bytes=32 * 1024 * 1024),
        name="scan_forward",
    )(x, raw, gate, sel, vec(bias), decay, vec(skip))


def scan_backward(x, raw, gate, y, grad, hist, sel, bias, decay, skip):
    seqs, length, channels = x.shape
    states_n = decay.shape[0]
    steps = chunk_steps(length)
    n = length // steps
    act = pl.BlockSpec((seqs, steps, channels), lambda i: (0, n - 1 - i, 0))
    selspec = pl.BlockSpec((seqs, steps // ROWS, 2 * states_n, ROWS), lambda i: (0, n - 1 - i, 0, 0))
    whole = lambda shape: pl.BlockSpec(shape, lambda i: (0,) * len(shape))
    vec = lambda v: v.reshape(1, -1)
    elems = seqs * length * channels * states_n
    full = jax.ShapeDtypeStruct((seqs, length, channels), jnp.float32)
    return pl.pallas_call(
        scan_backward_kernel,
        grid=(n,),
        in_specs=[act, act, act, act, act,
            pl.BlockSpec((seqs, steps, states_n, channels), lambda i: (0, n - 1 - i, 0, 0)),
            selspec, whole((1, channels)), whole(decay.shape), whole((1, channels))],
        out_specs=[act, act, act, selspec, whole(decay.shape), whole((ROWS, channels)), whole((ROWS, channels))],
        out_shape=[
            full, full, full,
            jax.ShapeDtypeStruct(sel.shape, jnp.float32),
            jax.ShapeDtypeStruct(decay.shape, jnp.float32),
            jax.ShapeDtypeStruct((ROWS, channels), jnp.float32),
            jax.ShapeDtypeStruct((ROWS, channels), jnp.float32),
        ],
        scratch_shapes=[pltpu.VMEM((seqs * channels // LANES, states_n, LANES), jnp.float32)],
        cost_estimate=pl.CostEstimate(flops=20 * elems, bytes_accessed=4 * elems, transcendentals=elems),
        compiler_params=pltpu.CompilerParams(vmem_limit_bytes=32 * 1024 * 1024),
        name="scan_backward",
    )(x, raw, gate, y, grad, hist, sel, vec(bias), decay, vec(skip))


def bit(axis):
    return lax.axis_index(axis)


def exchange(value, axis):
    return lax.ppermute(value, axis, SWAP)


def exchange_diagonal(value):
    return lax.ppermute(value, ("b", "x"), ((0, 3), (1, 2), (2, 1), (3, 0)))


def ordered(axis, mine, other):
    first = bit(axis) == 0
    return lax.select(first, mine, other), lax.select(first, other, mine)


def half_of(value, axis, other=False):
    width = value.shape[-1] // 2
    at = bit(axis) if not other else 1 - bit(axis)
    return lax.dynamic_slice_in_dim(value, at * width, width, axis=value.ndim - 1)


class Layout:
    def __init__(self, high):
        self.high = high
        self.sums = high + ("y",)

    def columns_in(self, value):
        lead = value.shape[:-1]
        k = len(self.high)
        value = value.reshape(lead + (2,) * (k + 2) + (-1,))
        base = len(lead)
        for place, axis in enumerate(self.high + ("b", "y")):
            if axis != "b":
                value = lax.select(bit(axis) == 0, value, lax.rev(value, (base + place,)))
        value = jnp.moveaxis(value, base + k + 1, base)
        return value.reshape(lead + (-1,))

    def columns_out(self, value):
        lead = value.shape[:-1]
        k = len(self.high)
        value = value.reshape(lead + (2,) * (k + 2) + (-1,))
        base = len(lead)
        value = jnp.moveaxis(value, base, base + k + 1)
        for place, axis in enumerate(self.high + ("b", "y")):
            if axis != "b":
                value = lax.select(bit(axis) == 0, value, lax.rev(value, (base + place,)))
        return value.reshape(lead + (-1,))

    def fetch(self, shard):
        mine = half_of(shard, "b")
        other = exchange(half_of(shard, "b", True), "b")
        pieces = [jnp.concatenate(ordered("b", mine, other), axis=0)]
        for axis in self.high[::-1] + ("y",):
            pieces = pieces + [exchange(piece, axis) for piece in pieces]
        return jnp.concatenate(pieces, axis=0)

    def settle(self, grad):
        total = grad
        for axis in ("y",) + self.high:
            rows = total.shape[0] // 2
            total = (total[:rows].astype(F32) + exchange(total[rows:], axis).astype(F32)).astype(BF)
        rows = total.shape[0] // 2
        low, high = total[:rows], total[rows:]
        keep, send = ordered("b", low, high)
        parts = ordered("b", keep, exchange(send, "b"))
        return jnp.concatenate(parts, axis=1).astype(F32)


def gather_rows(rows):
    beside = exchange(rows, "x")
    across = exchange(rows, "b")
    corner = exchange_diagonal(rows)
    mine = jnp.stack([jnp.stack([rows, beside]), jnp.stack([across, corner])])
    other = exchange(mine, "c")
    even, odd = ordered("c", mine, other)
    stacked = jnp.stack([even, odd], axis=2)
    left, right = ordered("x", stacked[:, 0], stacked[:, 1])
    return jnp.stack([left, right], axis=1).reshape(2 * QUARTERS * rows.shape[0], -1)


def gather_sequence(rows):
    even, odd = ordered("c", rows, exchange(rows, "c"))
    pair = jnp.stack([even, odd])
    left, right = ordered("x", pair, exchange(pair, "x"))
    return jnp.stack([left, right]).reshape(QUARTERS * rows.shape[0], -1)


def scatter_rows(partial):
    rows = partial.shape[0] // 8
    value = partial.reshape(2, 2, 2, rows, -1)
    mine = lax.dynamic_index_in_dim(value, bit("c"), 2, False)
    send = lax.dynamic_index_in_dim(value, 1 - bit("c"), 2, False)
    mine = mine + exchange(send.astype(BF), "c").astype(F32)
    here = lax.dynamic_index_in_dim(mine, bit("x"), 1, False)
    there = lax.dynamic_index_in_dim(mine, 1 - bit("x"), 1, False).astype(BF)
    beside = exchange(there[0], "x")
    across = exchange(here[1].astype(BF), "b")
    corner = exchange_diagonal(there[1])
    return here[0] + beside.astype(F32) + across.astype(F32) + corner.astype(F32)


def channel_total(partial):
    total = partial + exchange(partial, "c")
    total = total + exchange(total, "x")
    other = exchange(total, "b")
    rows = total.shape[0] // 2
    return total + jnp.concatenate([other[rows:], other[:rows]], axis=0)


def channel_return(partial):
    total = partial
    for axis in ("c", "x"):
        total = total + exchange(total.astype(BF), axis).astype(F32)
    other = exchange(total.astype(BF), "b").astype(F32)
    rows = total.shape[0] // 2
    return total + jnp.concatenate([other[rows:], other[:rows]], axis=0)


def rms(stream, gain_row):
    scale = lax.rsqrt(jnp.mean(stream * stream, axis=-1, keepdims=True) + EPS)
    return (stream * scale * gain_row[None, :]).astype(BF)


def rms_back(stream, gain_row, grad):
    scale = lax.rsqrt(jnp.mean(stream * stream, axis=-1, keepdims=True) + EPS)
    gain_grad = jnp.sum(grad * stream * scale, axis=0)
    scaled = grad * gain_row[None, :]
    inner = jnp.mean(scaled * stream, axis=-1, keepdims=True)
    return scale * scaled - stream * (scale * scale * scale * inner), gain_grad


def mm(left, right):
    return jnp.dot(left, right, preferred_element_type=F32)


def mm_nt(left, right):
    return lax.dot_general(left, right, (((1,), (1,)), ((), ())), preferred_element_type=F32)


def mm_tn(left, right):
    return lax.dot_general(left, right, (((0,), (0,)), ((), ())), preferred_element_type=F32)


def conv_total(inner, taps, bias):
    count, length = taps.shape[0], inner.shape[1]
    padded = jnp.pad(inner, ((0, 0), (count - 1, 0), (0, 0)))
    total = bias[None, None, :]
    for k in range(count):
        total = total + taps[k][None, None, :] * padded[:, k : k + length]
    return total


def conv_back(grad, inner, taps):
    count, length = taps.shape[0], inner.shape[1]
    before = jnp.pad(inner, ((0, 0), (count - 1, 0), (0, 0)))
    after = jnp.pad(grad, ((0, 0), (0, count - 1), (0, 0)))
    inner_grad = 0.0
    taps_grad = []
    for k in range(count):
        shift = count - 1 - k
        inner_grad = inner_grad + taps[k][None, None, :] * after[:, shift : shift + length]
        taps_grad.append(jnp.sum(grad * before[:, k : k + length], axis=(0, 1)))
    return inner_grad, jnp.stack(taps_grad), jnp.sum(grad, axis=(0, 1))


def mixer_forward(normed, weights, select_weight, step_weight, taps, conv_bias, step_bias, decay_log, skip_gain):
    inner_weight, gate_weight, out_weight = weights
    tokens = normed.shape[0]
    length = tokens // 2
    shaped = lambda v: v.reshape(2, length, -1)
    inner = shaped(mm(normed, inner_weight))
    gate = shaped(mm(normed, gate_weight))
    conv_out = jax.nn.silu(conv_total(inner, taps, conv_bias)).astype(BF)
    flat = conv_out.reshape(tokens, -1)
    selected = channel_total(mm_nt(flat, select_weight))
    rank = step_weight.shape[0]
    step_low = selected[:, :rank].astype(BF)
    raw = shaped(mm(step_low, step_weight))
    sel = selected[:, rank:].reshape(2, length // ROWS, ROWS, -1).transpose(0, 1, 3, 2)
    mixed, gated, hist = scan_forward(conv_out.astype(F32), raw, gate, sel, step_bias, decay_log, skip_gain)
    gated = gated.reshape(tokens, -1).astype(BF)
    partial = mm_nt(gated, out_weight)
    return partial, (normed, inner, gate, conv_out, step_low, raw, sel, mixed, gated, hist)


def mixer_backward(
    stored, low_grad, weights, select_weight, step_weight, taps, conv_bias, step_bias, decay_log, skip_gain
):
    inner_weight, gate_weight, out_weight = weights
    normed, inner, gate, conv_out, step_low, raw, sel, mixed, gated, hist = stored
    tokens = normed.shape[0]
    length = tokens // 2
    shaped = lambda v: v.reshape(2, length, -1)
    flat = lambda v: v.reshape(tokens, -1)
    out_grad = mm_tn(low_grad, gated).astype(BF)
    gated_grad = shaped(mm(low_grad, out_weight))
    gate_grad, conv_scan, raw_grad, sel_grad, decay_grad, skip_grad, bias_grad = scan_backward(
        conv_out.astype(F32), raw, gate, mixed, gated_grad, hist, sel, step_bias, decay_log, skip_gain
    )
    raw_low = flat(raw_grad).astype(BF)
    step_grad = mm_tn(step_low, raw_low)
    step_low_grad = mm_nt(raw_low, step_weight)
    states = sel_grad.transpose(0, 1, 3, 2).reshape(tokens, -1)
    select_low = channel_return(jnp.concatenate([step_low_grad, states], axis=1)).astype(BF)
    select_grad = mm_tn(select_low, flat(conv_out))
    conv_grad = conv_scan + shaped(mm(select_low, select_weight))
    before = conv_total(inner, taps, conv_bias)
    sig = jax.nn.sigmoid(before)
    inner_grad, taps_grad, conv_bias_grad = conv_back(conv_grad * sig * (1.0 + before * (1.0 - sig)), inner, taps)
    inner_low, gate_low = flat(inner_grad.astype(BF)), flat(gate_grad.astype(BF))
    partial = mm_nt(inner_low, inner_weight) + mm_nt(gate_low, gate_weight)
    matrices = (mm_tn(normed, inner_low).astype(BF), mm_tn(normed, gate_low).astype(BF), out_grad)
    small = jnp.concatenate(
        [
            select_grad,
            step_grad,
            taps_grad,
            conv_bias_grad[None],
            jnp.sum(bias_grad, axis=0, keepdims=True),
            decay_grad,
            jnp.sum(skip_grad, axis=0, keepdims=True),
        ],
        axis=0,
    )
    return partial, matrices, small


def ffn_forward(normed, weights):
    gate_weight, up_weight, down_weight = weights
    gate, up = mm(normed, gate_weight), mm(normed, up_weight)
    hidden = (jax.nn.silu(gate) * up).astype(BF)
    return mm_nt(hidden, down_weight), (normed, gate, up, hidden)


def ffn_backward(stored, low_grad, weights):
    gate_weight, up_weight, down_weight = weights
    normed, gate, up, hidden = stored
    hidden_grad = mm(low_grad, down_weight)
    sig = jax.nn.sigmoid(gate)
    gate_low = (hidden_grad * up * sig * (1.0 + gate * (1.0 - sig))).astype(BF)
    up_low = (hidden_grad * gate * sig).astype(BF)
    partial = mm_nt(gate_low, gate_weight) + mm_nt(up_low, up_weight)
    down_grad = mm_tn(low_grad, hidden).astype(BF)
    return partial, (mm_tn(normed, gate_low).astype(BF), mm_tn(normed, up_low).astype(BF), down_grad)


def rotate(values, direction):
    length, size_head = values.shape[1], values.shape[3]
    half_size = size_head // 2
    positions = jnp.arange(length, dtype=F32)
    frequency = ROPE_BASE ** (-jnp.arange(half_size, dtype=F32) * 2.0 / size_head)
    angles = positions[:, None] * frequency[None, :]
    cosine = jnp.cos(angles)[None, :, None, :]
    sine = direction * jnp.sin(angles)[None, :, None, :]
    first, second = values[..., :half_size], values[..., half_size:]
    return jnp.concatenate([first * cosine - second * sine, second * cosine + first * sine], axis=-1)


def masked_scores(queries, keys):
    length = queries.shape[1]
    rows_at = jnp.arange(length)[:, None]
    cols_at = jnp.arange(length)[None, :]
    mask = (cols_at <= rows_at) & (rows_at - cols_at < WINDOW)
    scores = jnp.einsum("sqhd,skhd->shqk", queries, keys, preferred_element_type=F32) * HEAD_DIM**-0.5
    return jnp.where(mask[None, None], scores, MASKED)


def attention_forward(normed, weights):
    in_weight, out_weight = weights
    tokens = normed.shape[0]
    width = in_weight.shape[1] // 3
    triple = mm(normed, in_weight)
    heads = lambda v: v.reshape(2, tokens // 2, width // HEAD_DIM, HEAD_DIM)
    queries = rotate(heads(triple[:, :width]), 1.0).astype(BF)
    keys = rotate(heads(triple[:, width : 2 * width]), 1.0).astype(BF)
    values = heads(triple[:, 2 * width :]).astype(BF)
    scores = masked_scores(queries, keys)
    peak = jnp.max(scores, axis=-1, keepdims=True)
    raised = jnp.exp(scores - peak)
    total = jnp.sum(raised, axis=-1, keepdims=True)
    attend = (raised / total).astype(BF)
    context = jnp.einsum("shqk,skhd->sqhd", attend, values, preferred_element_type=F32)
    context = context.reshape(tokens, width).astype(BF)
    return mm_nt(context, out_weight), (normed, queries, keys, values, peak + jnp.log(total), context)


def attention_backward(stored, low_grad, weights):
    in_weight, out_weight = weights
    normed, queries, keys, values, log_total, context = stored
    tokens = normed.shape[0]
    out_grad = mm_tn(low_grad, context).astype(BF)
    context_grad = mm(low_grad, out_weight).astype(BF).reshape(queries.shape)
    full = jnp.exp(masked_scores(queries, keys) - log_total)
    attend = full.astype(BF)
    value_grad = jnp.einsum("shqk,sqhd->skhd", attend, context_grad, preferred_element_type=F32)
    attend_grad = jnp.einsum("sqhd,skhd->shqk", context_grad, values, preferred_element_type=F32)
    row_delta = jnp.sum(full * attend_grad, axis=-1, keepdims=True)
    score_grad = (full * (attend_grad - row_delta)).astype(BF)
    query_grad = jnp.einsum("shqk,skhd->sqhd", score_grad, keys, preferred_element_type=F32) * HEAD_DIM**-0.5
    key_grad = jnp.einsum("shqk,sqhd->skhd", score_grad, queries, preferred_element_type=F32) * HEAD_DIM**-0.5
    flat = lambda v: v.reshape(tokens, -1)
    triple_low = jnp.concatenate(
        [flat(rotate(query_grad, -1.0)), flat(rotate(key_grad, -1.0)), flat(value_grad)], axis=1
    ).astype(BF)
    return mm_nt(triple_low, in_weight), (mm_tn(normed, triple_low).astype(BF), out_grad)


def shards(
    layout,
    layer_input,
    upstream,
    norm_gains,
    mixer_input,
    conv_taps,
    conv_bias,
    mixer_select,
    mixer_step,
    step_bias,
    decay_log,
    skip_gain,
    mixer_output,
    first_gate_up,
    first_down,
    attention_input,
    attention_output,
    second_gate_up,
    second_down,
):
    mine = lambda v: half_of(v, "b")
    fetch = layout.fetch
    dp_axes = layout.high + ("b", "y")
    quarter = bit("x") * 2 + bit("c")
    rows = layer_input.shape[0] // QUARTERS
    own_rows = lambda v: layout.columns_in(lax.dynamic_slice_in_dim(v, quarter * rows, rows, axis=0))
    gains = layout.columns_in(norm_gains)
    taps, bias_conv, bias_step, decay, skip = (mine(v) for v in (conv_taps, conv_bias, step_bias, decay_log, skip_gain))

    stream0 = own_rows(layer_input).astype(F32)
    normed0 = gather_rows(rms(stream0, gains[0]))
    mixer_weights = (fetch(mixer_input[:, 0]), fetch(mixer_input[:, 1]), fetch(mixer_output))
    select_weight = mine(lax.all_gather(mixer_select, dp_axes, axis=0, tiled=True))
    step_weight = mine(lax.all_gather(mixer_step, dp_axes, axis=0, tiled=True))
    channel = (taps, bias_conv, bias_step, decay, skip)
    partial, mixer_stored = mixer_forward(normed0, mixer_weights, select_weight, step_weight, *channel)
    stream1 = stream0 + scatter_rows(partial)

    first_weights = (fetch(first_gate_up[:, 0]), fetch(first_gate_up[:, 1]), fetch(first_down))
    partial, first_stored = ffn_forward(gather_rows(rms(stream1, gains[1])), first_weights)
    stream2 = stream1 + scatter_rows(partial)

    rows_here = attention_input.shape[0]
    half = attention_input.shape[2] // 2
    triple = attention_input.reshape(rows_here, 3, 2, half).transpose(0, 2, 1, 3).reshape(rows_here, -1)
    attention_weights = (fetch(triple), fetch(attention_output))
    partial, attention_stored = attention_forward(gather_rows(rms(stream2, gains[2])), attention_weights)
    stream3 = stream2 + scatter_rows(partial)

    second_weights = (fetch(second_gate_up[:, 0]), fetch(second_gate_up[:, 1]), fetch(second_down))
    partial, second_stored = ffn_forward(gather_rows(rms(stream3, gains[3])), second_weights)
    stream4 = stream3 + scatter_rows(partial)
    layer_output = gather_sequence(layout.columns_out(stream4.astype(BF)))

    upstream_rows = own_rows(upstream)
    grad4 = upstream_rows.astype(F32)
    partial, second_grads = ffn_backward(second_stored, gather_rows(upstream_rows), second_weights)
    back, gain3 = rms_back(stream3, gains[3], scatter_rows(partial))
    grad3 = grad4 + back
    partial, attention_grads = attention_backward(attention_stored, gather_rows(grad3.astype(BF)), attention_weights)
    back, gain2 = rms_back(stream2, gains[2], scatter_rows(partial))
    grad2 = grad3 + back
    partial, first_grads = ffn_backward(first_stored, gather_rows(grad2.astype(BF)), first_weights)
    back, gain1 = rms_back(stream1, gains[1], scatter_rows(partial))
    grad1 = grad2 + back
    partial, mixer_grads, small = mixer_backward(
        mixer_stored, gather_rows(grad1.astype(BF)), mixer_weights, select_weight, step_weight, *channel
    )
    back, gain0 = rms_back(stream0, gains[0], scatter_rows(partial))
    input_grad = gather_sequence(layout.columns_out(grad1 + back))

    settle = layout.settle
    second_out = [settle(g) for g in second_grads]
    attention_out = [settle(g) for g in attention_grads]
    first_out = [settle(g) for g in first_grads]
    mixer_out = [settle(g) for g in mixer_grads]
    pair = lambda parts: jnp.stack(parts, axis=1)

    for axis in layout.sums:
        small = small + exchange(small.astype(BF), axis).astype(F32)
    small = jnp.concatenate(ordered("b", small, exchange(small.astype(BF), "b").astype(F32)), axis=1)
    dp_index = lax.axis_index(dp_axes)
    select_rows, step_rows = mixer_select.shape[0], mixer_step.shape[0]
    select_all, step_all = select_weight.shape[0], step_weight.shape[0]
    select_grad = lax.dynamic_slice_in_dim(small[:select_all], dp_index * select_rows, select_rows, axis=0)
    step_grad = lax.dynamic_slice_in_dim(
        small[select_all : select_all + step_all], dp_index * step_rows, step_rows, axis=0
    )
    rest = small[select_all + step_all :]
    count, states_n = conv_taps.shape[0], decay_log.shape[0]
    taps_grad, conv_bias_grad, step_bias_grad = rest[:count], rest[count], rest[count + 1]
    decay_grad, skip_grad = rest[count + 2 : count + 2 + states_n], rest[count + 2 + states_n]

    gains_grad = layout.columns_out(jnp.stack([gain0, gain1, gain2, gain3]))
    for axis in ("c", "x", "b", "y") + layout.high:
        gains_grad = gains_grad + exchange(gains_grad, axis)

    triple_grad = attention_out[0].reshape(rows_here, 2, 3, half).transpose(0, 2, 1, 3).reshape(attention_input.shape)
    return (
        layer_output,
        input_grad,
        gains_grad,
        pair(mixer_out[:2]),
        taps_grad,
        conv_bias_grad,
        select_grad,
        step_grad,
        step_bias_grad,
        decay_grad,
        skip_grad,
        mixer_out[2],
        pair(first_out[:2]),
        first_out[2],
        triple_grad,
        attention_out[1],
        pair(second_out[:2]),
        second_out[2],
    )


def solution(mesh):
    n_dp, n_tensor = mesh.devices.shape
    bits = n_dp.bit_length() - 1
    assert n_dp == 1 << bits and bits >= 2 and n_tensor == 4
    high = tuple("a%d" % k for k in range(bits - 2))
    names = high + ("b", "y", "x", "c")
    cube = jax.sharding.Mesh(mesh.devices.reshape((2,) * len(names)), names)
    dp, tensor = high + ("b", "y"), ("x", "c")
    row, both, col = P(dp, None), P(dp, tensor), P(None, tensor)
    three, vec = P(dp, None, tensor), P(tensor)
    return jax.shard_map(
        functools.partial(shards, Layout(high)),
        mesh=cube,
        in_specs=(
            row, row, P(), three, col, vec, both, both, vec, col, vec, both, three, both, three, both, three, both,
        ),
        out_specs=(
            row, row, P(), three, col, vec, both, both, vec, col, vec, both, three, both, three, both, three, both,
        ),
        check_vma=False,
    )
```

```python
import functools
import jax
import jax.numpy as jnp
from jax import lax
from jax.experimental import pallas as pl
from jax.experimental.pallas import tpu as pltpu
from jax.sharding import PartitionSpec as P

HEAD_DIM = 64
WINDOW = 2048
EPS = 1e-05
ROPE_BASE = 10000.0
MASKED = -1e30
BF = jnp.bfloat16
F32 = jnp.float32
SWAP = ((0, 1), (1, 0))
QUARTERS = 4
LANES = 128
ROWS = 8


def scan_forward_kernel(
    place_ref, x_ref, raw_ref, gate_ref, sel_ref, bias_ref, decay_ref, skip_ref, y_ref, gated_ref, hist_ref, state_ref
):
    seqs, steps, channels = x_ref.shape
    blocks = channels // LANES
    states_n = decay_ref.shape[0]
    pairs = [(s, j) for s in range(seqs) for j in range(blocks)]

    @pl.when(pl.program_id(1) == 0)
    def _():
        state_ref[...] = jnp.zeros_like(state_ref)

    def lanes(j):
        return slice(j * LANES, (j + 1) * LANES)

    rates = [-jnp.exp(decay_ref[:, lanes(j)]) for j in range(blocks)]

    def chunk(k, states):
        states = list(states)
        rows = pl.ds(pl.multiple_of(k * ROWS, ROWS), ROWS)
        x_t, d_t, dx_t = {}, {}, {}
        for s, j in pairs:
            x_t[s, j] = x_ref[s, rows, lanes(j)]
            d_t[s, j] = jax.nn.softplus(raw_ref[s, rows, lanes(j)] + bias_ref[:, lanes(j)])
            dx_t[s, j] = d_t[s, j] * x_t[s, j]
        outs = {p: [] for p in pairs}
        for i in range(ROWS):
            for s in range(seqs):
                sel_b = jnp.broadcast_to(sel_ref[s, k, :states_n, i : i + 1], (states_n, LANES))
                sel_c = jnp.broadcast_to(sel_ref[s, k, states_n:, i : i + 1], (states_n, LANES))
                for j in range(blocks):
                    at = s * blocks + j
                    before = states[at]
                    hist_ref[s, k * ROWS + i, :, lanes(j)] = before
                    factor = jnp.exp(d_t[s, j][i : i + 1] * rates[j])
                    after = factor * before + dx_t[s, j][i : i + 1] * sel_b
                    states[at] = after
                    outs[s, j].append(jnp.sum(after * sel_c, axis=0, keepdims=True))
        for s, j in pairs:
            y = jnp.concatenate(outs[s, j], axis=0) + skip_ref[:, lanes(j)] * x_t[s, j]
            gate = gate_ref[0, s, 0, rows, lanes(j)]
            y_ref[s, rows, lanes(j)] = y
            gated_ref[0, s, 0, rows, lanes(j)] = y * gate * jax.nn.sigmoid(gate)
        return tuple(states)

    first = tuple(state_ref[s * blocks + j] for s, j in pairs)
    last = lax.fori_loop(0, steps // ROWS, chunk, first)
    for at, value in enumerate(last):
        state_ref[at] = value


def group_sums(states_n):
    shape = (ROWS, ROWS * states_n)
    step = lax.broadcasted_iota(jnp.int32, shape, 1) // states_n
    return (step == lax.broadcasted_iota(jnp.int32, shape, 0)).astype(jnp.bfloat16)


def scan_backward_kernel(
    place_ref, x_ref, raw_ref, gate_ref, y_ref, grad_ref, hist_ref, sel_ref, bias_ref, decay_ref, skip_ref,
    dgate_ref, dx_ref, draw_ref, dsel_ref, ddecay_ref, dskip_ref, dbias_ref,
    adj_ref, step_ref, drive_ref, out_ref, first_ref, second_ref, db_ref, dc_ref,
):
    _, steps, channels = x_ref.shape
    blocks = channels // LANES
    states_n = decay_ref.shape[0]

    @pl.when(pl.program_id(1) == 0)
    def _():
        adj_ref[...] = jnp.zeros_like(adj_ref)

    @pl.when((pl.program_id(0) == 0) & (pl.program_id(1) == 0))
    def _():
        ddecay_ref[...] = jnp.zeros_like(ddecay_ref)
        dskip_ref[...] = jnp.zeros_like(dskip_ref)
        dbias_ref[...] = jnp.zeros_like(dbias_ref)

    def lanes(j):
        return slice(j * LANES, (j + 1) * LANES)

    rates = [-jnp.exp(decay_ref[:, lanes(j)]) for j in range(blocks)]
    sums = group_sums(states_n)
    ones = jnp.ones((ROWS, LANES), jnp.bfloat16)
    over_lanes = lambda v: lax.dot_general(ones, v, (((1,), (1,)), ((), ())), preferred_element_type=jnp.float32)

    def chunk(step, carry):
        adjoint, decay_sum = list(carry[0]), list(carry[1])
        k = steps // ROWS - 1 - step
        rows = pl.ds(pl.multiple_of(k * ROWS, ROWS), ROWS)
        x = x_ref[0, rows, :]
        z = raw_ref[0, rows, :] + bias_ref[...]
        delta = jax.nn.softplus(z)
        gate = gate_ref[0, 0, 0, rows, :]
        sig = jax.nn.sigmoid(gate)
        grad = grad_ref[0, 0, 0, rows, :]
        dy = grad * gate * sig
        dgate_ref[0, 0, 0, rows, :] = grad * y_ref[0, rows, :] * sig * (1.0 + gate * (1.0 - sig))
        step_ref[...] = delta
        drive_ref[...] = delta * x
        out_ref[...] = dy
        for i in reversed(range(ROWS)):
            place = slice(i * states_n, (i + 1) * states_n)
            sel_b = jnp.broadcast_to(sel_ref[0, k, :states_n, i : i + 1], (states_n, LANES))
            sel_c = jnp.broadcast_to(sel_ref[0, k, states_n:, i : i + 1], (states_n, LANES))
            db = jnp.zeros((states_n, LANES), jnp.float32)
            dc = jnp.zeros((states_n, LANES), jnp.float32)
            for j in range(blocks):
                before = hist_ref[0, k * ROWS + i, :, lanes(j)]
                width = step_ref[i : i + 1, lanes(j)]
                drive = drive_ref[i : i + 1, lanes(j)]
                out = out_ref[i : i + 1, lanes(j)]
                factor = jnp.exp(width * rates[j])
                after = factor * before + drive * sel_b
                lam = adjoint[j] + out * sel_c
                dc = dc + out * after
                db = db + drive * lam
                first_ref[place, lanes(j)] = (lam * sel_b).astype(jnp.bfloat16)
                back = lam * factor
                adjoint[j] = back
                through = back * before
                second_ref[place, lanes(j)] = (rates[j] * through).astype(jnp.bfloat16)
                decay_sum[j] = decay_sum[j] + width * through
            db_ref[place, :] = db.astype(jnp.bfloat16)
            dc_ref[place, :] = dc.astype(jnp.bfloat16)
        dsel_ref[0, k, 0:ROWS, :] = over_lanes(db_ref[...])
        dsel_ref[0, k, ROWS : 2 * ROWS, :] = over_lanes(dc_ref[...])
        one = jnp.dot(sums, first_ref[...], preferred_element_type=jnp.float32)
        two = jnp.dot(sums, second_ref[...], preferred_element_type=jnp.float32)
        dx_ref[0, rows, :] = dy * skip_ref[...] + delta * one
        draw = (two + x * one) * jax.nn.sigmoid(z)
        draw_ref[0, rows, :] = draw
        dskip_ref[...] += dy * x
        dbias_ref[...] += draw
        return tuple(adjoint), tuple(decay_sum)

    carry = (
        tuple(adj_ref[j] for j in range(blocks)),
        tuple(jnp.zeros((states_n, LANES), jnp.float32) for _ in range(blocks)),
    )
    adjoint, decay_sum = lax.fori_loop(0, steps // ROWS, chunk, carry, unroll=2)
    for j in range(blocks):
        adj_ref[j] = adjoint[j]
        ddecay_ref[:, lanes(j)] += rates[j] * decay_sum[j]


def quarter_block(place, quarter):
    return place[1] ^ (quarter & 1), place[0] ^ (quarter >> 1)


def scan_call(kernel, name, ins, outs, sel, vectors, place, reverse, extra_outs=(), scratch=()):
    seqs, length, channels = ins[0][1].shape
    states_n = vectors[1].shape[0]
    steps = length // QUARTERS
    turn = lambda i: QUARTERS - 1 - i if reverse else i

    def spec(kind, width):
        if kind == "time":
            return pl.BlockSpec((1, steps, width), lambda s, i, place: (s, turn(i), 0))
        if kind == "hist":
            return pl.BlockSpec((1, steps, states_n, width), lambda s, i, place: (s, turn(i), 0, 0))
        if kind == "dsel":
            return pl.BlockSpec((1, steps // ROWS, 2 * ROWS, ROWS * states_n), lambda s, i, place: (s, turn(i), 0, 0))
        if kind == "sel":
            return pl.BlockSpec((1, steps // ROWS, 2 * states_n, ROWS), lambda s, i, place: (s, turn(i), 0, 0))
        return pl.BlockSpec(
            (1, 1, 1, steps, width),
            lambda s, i, place: (quarter_block(place, turn(i))[0], s, quarter_block(place, turn(i))[1], 0, 0),
        )

    whole = lambda shape: pl.BlockSpec(shape, lambda s, i, place: (0,) * len(shape))
    shape_of = {
        "time": (seqs, length, channels),
        "hist": (seqs, length, states_n, channels),
        "dsel": sel.shape[:2] + (2 * ROWS, ROWS * states_n),
        "mine": (2, seqs, 2, steps, channels),
    }
    elems = seqs * length * channels * states_n
    full = lambda shape: jax.ShapeDtypeStruct(shape, jnp.float32)
    return pl.pallas_call(
        kernel,
        grid_spec=pltpu.PrefetchScalarGridSpec(
            num_scalar_prefetch=1,
            grid=(seqs, QUARTERS),
            in_specs=[spec(kind, channels) for kind, _ in ins] + [spec("sel", 0)] + [whole(v.shape) for v in vectors],
            out_specs=[spec(kind, channels) for kind in outs] + [whole(shape) for shape in extra_outs],
            scratch_shapes=[pltpu.VMEM((channels // LANES, states_n, LANES), jnp.float32)] + list(scratch),
        ),
        out_shape=[full(shape_of[kind]) for kind in outs] + [full(shape) for shape in extra_outs],
        cost_estimate=pl.CostEstimate(
            flops=(60 if reverse else 20) * elems, bytes_accessed=4 * elems, transcendentals=elems
        ),
        compiler_params=pltpu.CompilerParams(vmem_limit_bytes=48 * 1024 * 1024),
        name=name,
    )(place, *[v for _, v in ins], sel, *vectors)


def scan_forward(x, raw, gate, sel, bias, decay, skip, place):
    ins = (("time", x), ("time", raw), ("mine", gate))
    vectors = (bias.reshape(1, -1), decay, skip.reshape(1, -1))
    return scan_call(scan_forward_kernel, "scan_forward", ins, ("time", "mine", "hist"), sel, vectors, place, False)


def scan_backward(x, raw, gate, y, grad, hist, sel, bias, decay, skip, place):
    ins = (("time", x), ("time", raw), ("mine", gate), ("time", y), ("mine", grad), ("hist", hist))
    vectors = (bias.reshape(1, -1), decay, skip.reshape(1, -1))
    extra = (decay.shape, (ROWS, x.shape[2]), (ROWS, x.shape[2]))
    group, channels = ROWS * decay.shape[0], x.shape[2]
    scratch = (
        [pltpu.VMEM((ROWS, channels), jnp.float32)] * 3
        + [pltpu.VMEM((group, channels), jnp.bfloat16)] * 2
        + [pltpu.VMEM((group, LANES), jnp.bfloat16)] * 2
    )
    outs = ("mine", "time", "time", "dsel")
    return scan_call(scan_backward_kernel, "scan_backward", ins, outs, sel, vectors, place, True, extra, scratch)


def turn_heads(value, cosine, sine):
    size = value.shape[1]
    half = HEAD_DIM // 2
    lane = lax.broadcasted_iota(jnp.int32, value.shape, 1)
    partner = jnp.where(lane % HEAD_DIM < half, pltpu.roll(value, size - half, 1), pltpu.roll(value, half, 1))
    return value * cosine + partner * sine


def head_pair(ref, part, pair, pairs):
    at = (part * pairs + pair) * LANES
    return ref[:, 0, :, :, at : at + LANES].reshape(-1, LANES)


def pair_weights(queries, keys, head_lanes, mask):
    zero = jnp.zeros_like(queries)
    scores = lax.dot_general(
        jnp.where(head_lanes, queries, zero), keys, (((1,), (1,)), ((), ())), preferred_element_type=jnp.float32
    )
    scores = jnp.where(mask, scores * HEAD_DIM**-0.5, MASKED)
    raised = jnp.exp(scores - jnp.max(scores, axis=1, keepdims=True))
    return raised / jnp.sum(raised, axis=1, keepdims=True)


def attention_forward_kernel(triple_ref, cos_ref, sin_ref, row_ref, col_ref, turned_ref, context_ref):
    pairs = context_ref.shape[-1] // LANES
    shape = context_ref.shape[:-1] + (LANES,)
    mask = (col_ref[...] <= row_ref[...]) & (row_ref[...] - col_ref[...] < WINDOW)
    cosine, sine = cos_ref[...], sin_ref[...]
    low_lanes = lax.broadcasted_iota(jnp.int32, (1, LANES), 1) < HEAD_DIM
    for pair in range(pairs):
        queries = turn_heads(head_pair(triple_ref, 0, pair, pairs), cosine, sine).astype(jnp.bfloat16)
        keys = turn_heads(head_pair(triple_ref, 1, pair, pairs), cosine, sine).astype(jnp.bfloat16)
        values = head_pair(triple_ref, 2, pair, pairs).astype(jnp.bfloat16)
        outs = []
        for head in range(LANES // HEAD_DIM):
            lanes = low_lanes if head == 0 else ~low_lanes
            attend = pair_weights(queries, keys, lanes, mask).astype(jnp.bfloat16)
            outs.append(jnp.dot(attend, values, preferred_element_type=jnp.float32))
        context = jnp.where(low_lanes, outs[0], outs[1]).astype(jnp.bfloat16)
        context_ref[..., pair * LANES : (pair + 1) * LANES] = context.reshape(shape)
        for part, value in enumerate((queries, keys, values)):
            at = (part * pairs + pair) * LANES
            turned_ref[..., at : at + LANES] = value.reshape(shape)


def attention_backward_kernel(turned_ref, grad_ref, cos_ref, sin_ref, row_ref, col_ref, out_ref):
    pairs = grad_ref.shape[-1] // LANES
    shape = grad_ref.shape[:-1] + (LANES,)
    mask = (col_ref[...] <= row_ref[...]) & (row_ref[...] - col_ref[...] < WINDOW)
    cosine, sine = cos_ref[...], -sin_ref[...]
    low_lanes = lax.broadcasted_iota(jnp.int32, (1, LANES), 1) < HEAD_DIM
    dot = lambda a, b, dims: lax.dot_general(a, b, (dims, ((), ())), preferred_element_type=jnp.float32)
    for pair in range(pairs):
        queries, keys, values = (head_pair(turned_ref, part, pair, pairs) for part in range(3))
        grads = head_pair(grad_ref, 0, pair, pairs)
        parts = [[], [], []]
        for head in range(LANES // HEAD_DIM):
            lanes = low_lanes if head == 0 else ~low_lanes
            full = pair_weights(queries, keys, lanes, mask)
            attend = full.astype(jnp.bfloat16)
            own = jnp.where(lanes, grads, jnp.zeros_like(grads))
            weight_grad = dot(own, values, ((1,), (1,)))
            delta = jnp.sum(full * weight_grad, axis=1, keepdims=True)
            score_grad = (full * (weight_grad - delta)).astype(jnp.bfloat16)
            parts[0].append(dot(score_grad, keys, ((1,), (0,))) * HEAD_DIM**-0.5)
            parts[1].append(dot(score_grad, queries, ((0,), (0,))) * HEAD_DIM**-0.5)
            parts[2].append(dot(attend, grads, ((0,), (0,))))
        for part, (low, high) in enumerate(parts):
            value = jnp.where(low_lanes, low, high)
            if part < 2:
                value = turn_heads(value, cosine, sine)
            at = (part * pairs + pair) * LANES
            out_ref[..., at : at + LANES] = value.astype(jnp.bfloat16).reshape(shape)


def rotary_tables(positions):
    half = HEAD_DIM // 2
    frequency = ROPE_BASE ** (-jnp.arange(half, dtype=F32) * 2.0 / HEAD_DIM)
    angles = positions.astype(F32)[:, None] * frequency[None, :]
    cosine, sine = jnp.cos(angles), jnp.sin(angles)
    twice = lambda low, high: jnp.concatenate([low, high] * (LANES // HEAD_DIM), axis=1)
    return twice(cosine, cosine), twice(-sine, sine), positions[:, None], positions[None, :]


def attention_call(kernel, name, ins, widths, tables):
    lead = ins[0].shape[:-1]
    split = lambda width: pl.BlockSpec((lead[0], 1) + lead[2:] + (width,), lambda s: (0, s, 0, 0, 0))
    whole = lambda a: pl.BlockSpec(a.shape, lambda s: (0, 0))
    length = lead[0] * lead[2] * lead[3]
    heads = widths[-1] // HEAD_DIM
    flops = 2 * lead[1] * 2 * length * length * LANES * 5 * max(heads, 1)
    return pl.pallas_call(
        kernel,
        grid=(lead[1],),
        in_specs=[split(a.shape[-1]) for a in ins] + [whole(t) for t in tables],
        out_specs=[split(w) for w in widths],
        out_shape=[jax.ShapeDtypeStruct(lead + (w,), jnp.bfloat16) for w in widths],
        cost_estimate=pl.CostEstimate(flops=flops, bytes_accessed=4 * 1024 * 1024, transcendentals=length * length * 8),
        compiler_params=pltpu.CompilerParams(vmem_limit_bytes=32 * 1024 * 1024),
        name=name,
    )(*ins, *tables)


def bit(axis):
    return lax.axis_index(axis)


def exchange(value, axis):
    return lax.ppermute(value, axis, SWAP)


def exchange_diagonal(value):
    return lax.ppermute(value, ("b", "x"), ((0, 3), (1, 2), (2, 1), (3, 0)))


def ordered(axis, mine, other):
    first = bit(axis) == 0
    return lax.select(first, mine, other), lax.select(first, other, mine)


def half_of(value, axis, other=False):
    width = value.shape[-1] // 2
    at = bit(axis) if not other else 1 - bit(axis)
    return lax.dynamic_slice_in_dim(value, at * width, width, axis=value.ndim - 1)


def tied(value, *tokens):
    return lax.optimization_barrier((value,) + tokens)[0]


class Pump:
    def __init__(self, layout):
        self.layout, self.waiting, self.flying = layout, [], []

    def add(self, job):
        self.waiting.append(job)

    def land(self, token):
        token, flying = lax.optimization_barrier((token, [results for _, results in self.flying]))
        self.flying = [(job, results) for (job, _), results in zip(self.flying, flying)]
        return token

    def turn(self, token, count=1, hold=0):
        split = len(self.flying) - hold
        going, held = self.flying[:split], self.flying[split:]
        if going:
            flat = [r for _, results in going for r in results]
            tied_all = lax.optimization_barrier((token, *flat))
            token, flat = tied_all[0], list(tied_all[1:])
        asks = []
        for job, results in going:
            got, flat = flat[: len(results)], flat[len(results) :]
            try:
                asks.append((job, job.send(got)))
            except StopIteration:
                pass
        for job in self.waiting[:count]:
            asks.append((job, [(tied(v, token), axis) for v, axis in next(job)]))
        del self.waiting[:count]
        self.flying = held + [(job, [exchange(v, axis) for v, axis in ask]) for job, ask in asks]
        return token

    def begin(self, token, count=1):
        for job in self.waiting[:count]:
            self.flying.append((job, [exchange(tied(v, token), axis) for v, axis in next(job)]))
        del self.waiting[:count]

    def until(self, token, store, *names):
        while not all(name in store for name in names):
            token = self.turn(token)
        return token

    def flush(self):
        jobs = [(job, [exchange(v, axis) for v, axis in next(job)]) for job in self.waiting]
        for job, results in self.flying + jobs:
            try:
                while True:
                    results = [exchange(v, axis) for v, axis in job.send(list(results))]
            except StopIteration:
                pass
        self.waiting, self.flying = [], []


class Layout:
    def __init__(self, high):
        self.high = high
        self.sums = high + ("y",)

    def split_bits(self, value, at):
        k = len(self.high) + 2
        return value.reshape(value.shape[:at] + (2,) * k + (value.shape[at] >> k,) + value.shape[at + 1 :])

    def turned(self, value, at):
        for place, axis in enumerate(self.high + ("b", "y")):
            if axis != "b":
                value = lax.select(bit(axis) == 0, value, lax.rev(value, (at + place,)))
        return value

    def columns_in(self, value, at=-1):
        shape, at = value.shape, at % value.ndim
        value = self.turned(self.split_bits(value, at), at)
        return jnp.moveaxis(value, at + len(self.high) + 1, at).reshape(shape)

    def columns_out(self, value, at=-1):
        shape, at = value.shape, at % value.ndim
        value = jnp.moveaxis(self.split_bits(value, at), at, at + len(self.high) + 1)
        return self.turned(value, at).reshape(shape)


def fetch_job(layout, mine, other, store, name):
    own = jnp.concatenate(ordered("b", mine, other), axis=0)
    axes = layout.high[::-1]
    if len(axes) == 1:
        high, beside = yield [(own, axes[0]), (own, "y")]
        (far,) = yield [(high, "y")]
        pieces = [own, high, beside, far]
    else:
        pieces = [own]
        for axis in axes + ("y",):
            got = yield [(piece, axis) for piece in pieces]
            pieces = pieces + list(got)
    store[name] = jnp.concatenate(pieces, axis=0)


def settle_job(layout, left, right, store, name):
    width = left.shape[1]
    got = []
    product = lambda lo, hi: sum((g[lo:hi].astype(F32) for g in got), mm_tn(left[:, lo:hi], right))
    for axis in ("y",) + layout.high:
        width = width // 2
        got += yield [(product(width, 2 * width).astype(BF), axis)]
    total = product(0, width).astype(BF)
    keep, send = ordered("b", total[: width // 2], total[width // 2 :])
    (other,) = yield [(send, "b")]
    store[name] = ordered("b", keep, other)


def small_job(layout, value, store, name):
    for axis in layout.sums:
        (got,) = yield [(value.astype(BF), axis)]
        value = value + got.astype(F32)
    (got,) = yield [(value.astype(BF), "b")]
    store[name] = jnp.concatenate(ordered("b", value, got.astype(F32)), axis=1)


def gather_rows(rows):
    with jax.named_scope("rows_gather"):
        beside = exchange(rows, "x")
        across = exchange(rows, "b")
        corner = exchange_diagonal(rows)
        mine = jnp.concatenate([rows, beside, across, corner], axis=-2)
        return jnp.concatenate([mine, exchange(mine, "c")], axis=-2)


def scatter_rows(products):
    with jax.named_scope("rows_scatter"):
        half = products[0][0].shape[0] // 2
        send = sum(mm_nt(v[half:], w) for v, w in products).astype(BF)
        got = exchange(send, "c")
        keep = sum(mm_nt(v[:half], w) for v, w in products) + got.astype(F32)
        rows = half // 4
        low = keep[rows:].astype(BF)
        beside = exchange(low[:rows], "x")
        across = exchange(low[rows : 2 * rows], "b")
        corner = exchange_diagonal(low[2 * rows :])
        return keep[:rows] + beside.astype(F32) + across.astype(F32) + corner.astype(F32)


def in_time(value):
    left, right = ordered("x", value[:, :, 0], value[:, :, 1])
    halves = [jnp.stack(ordered("c", half[0], half[1]), axis=1) for half in (left, right)]
    return jnp.stack(halves, axis=1).reshape(value.shape[1], -1, value.shape[-1])


def from_time(value, rows):
    value = value.reshape(value.shape[0], 2, 2, rows, value.shape[-1])
    parts = [jnp.stack(ordered("x", v[:, 0], v[:, 1]), axis=1) for v in ordered("c", value[:, :, 0], value[:, :, 1])]
    return jnp.stack(parts)


def gather_sequence(rows):
    even, odd = ordered("c", rows, exchange(rows, "c"))
    pair = jnp.stack([even, odd])
    left, right = ordered("x", pair, exchange(pair, "x"))
    return jnp.stack([left, right]).reshape(QUARTERS * rows.shape[0], -1)


def channel_total(partial, low=False):
    narrow = (lambda v: v.astype(BF)) if low else (lambda v: v)
    total = partial + exchange(narrow(partial), "c").astype(F32)
    return chip_total(total, narrow)


def chip_total(total, narrow=lambda v: v.astype(BF)):
    total = total + exchange(narrow(total), "x").astype(F32)
    other = exchange(narrow(total), "b").astype(F32)
    rows = total.shape[0] // 2
    return total + jnp.concatenate([other[rows:], other[:rows]], axis=0)


def rms(stream, gain_row):
    scale = lax.rsqrt(jnp.mean(stream * stream, axis=-1, keepdims=True) + EPS)
    return (stream * scale * gain_row[None, :]).astype(BF)


def rms_back(stream, gain_row, grad):
    scale = lax.rsqrt(jnp.mean(stream * stream, axis=-1, keepdims=True) + EPS)
    gain_grad = jnp.sum(grad * stream * scale, axis=0)
    scaled = grad * gain_row[None, :]
    inner = jnp.mean(scaled * stream, axis=-1, keepdims=True)
    return scale * scaled - stream * (scale * scale * scale * inner), gain_grad


def mm(left, right):
    return jnp.dot(left, right, preferred_element_type=F32)


def mm_nt(left, right):
    return lax.dot_general(left, right, (((1,), (1,)), ((), ())), preferred_element_type=F32)


def mm_tn(left, right):
    return lax.dot_general(left, right, (((0,), (0,)), ((), ())), preferred_element_type=F32)


def conv_total(inner, taps, bias):
    count, length = taps.shape[0], inner.shape[1]
    padded = jnp.pad(inner, ((0, 0), (count - 1, 0), (0, 0)))
    total = bias[None, None, :]
    for k in range(count):
        total = total + taps[k][None, None, :] * padded[:, k : k + length]
    return total


def conv_back(grad, inner, taps):
    count, length = taps.shape[0], inner.shape[1]
    before = jnp.pad(inner, ((0, 0), (count - 1, 0), (0, 0)))
    after = jnp.pad(grad, ((0, 0), (0, count - 1), (0, 0)))
    inner_grad = 0.0
    taps_grad = []
    for k in range(count):
        shift = count - 1 - k
        inner_grad = inner_grad + taps[k][None, None, :] * after[:, shift : shift + length]
        taps_grad.append(jnp.sum(grad * before[:, k : k + length], axis=(0, 1)))
    return inner_grad, jnp.stack(taps_grad), jnp.sum(grad, axis=(0, 1))


def mixer_backward(stored, low_grad, weights, channel, place, pump, store):
    inner_weight, gate_weight, out_weight, select_weight, step_weight = weights
    taps, conv_bias, step_bias, decay_log, skip_gain = channel
    normed, inner, gate, conv_out, step_low, raw, sel, mixed, gated, hist = stored
    tokens = normed.shape[0]
    rows = tokens // 8
    flat = lambda v: v.reshape(tokens, -1)
    gated_grad = mm(low_grad, out_weight)
    gated_grad = gated_grad.reshape(gate.shape)
    from_scan = scan_backward(
        conv_out.astype(F32), raw, gate, mixed, gated_grad, hist, sel, step_bias, decay_log, skip_gain, place
    )
    gate_grad, conv_scan, raw_grad, sel_grad, decay_grad, skip_grad, bias_grad = pump.land(tuple(from_scan))

    raw_low = flat(raw_grad).astype(BF)
    step_low_grad = mm_nt(raw_low, step_weight)
    states = [sel_grad[:, :, at].reshape(tokens, -1) for at in (0, ROWS)]
    select_grads = jnp.concatenate([step_low_grad, *states], axis=1)
    gate_low = flat(gate_grad.astype(BF))
    pump.add(settle_job(pump.layout, normed, gate_low, store, "gate"))
    with jax.named_scope("select_return"):
        select_grads = select_grads + exchange(select_grads.astype(BF), "c").astype(F32)
        select_grads = pump.turn(select_grads, 1)
        select_low = chip_total(select_grads).astype(BF)
    select_low = pump.turn(select_low, 0)
    conv_grad = conv_scan + mm(select_low, select_weight).reshape(conv_scan.shape)
    before = conv_total(inner, taps, conv_bias)
    sig = jax.nn.sigmoid(before)
    inner_grad, taps_grad, conv_bias_grad = conv_back(conv_grad * sig * (1.0 + before * (1.0 - sig)), inner, taps)
    inner_low = flat(from_time(inner_grad.astype(BF), rows))
    cut = inner_low.shape[1] // 2
    inner_parts = (inner_low[:, :cut], inner_low[:, cut:])
    for name, part in zip(("inner0", "inner1"), inner_parts):
        pump.add(settle_job(pump.layout, normed, part, store, name))
    small = jnp.concatenate(
        [
            mm_tn(select_low, flat(conv_out)),
            mm_tn(step_low, raw_low),
            taps_grad,
            conv_bias_grad[None],
            jnp.sum(bias_grad, axis=0, keepdims=True),
            decay_grad,
            jnp.sum(skip_grad, axis=0, keepdims=True),
        ],
        axis=0,
    )
    pump.add(small_job(pump.layout, small, store, "small"))
    pump.begin(inner_low, 3)
    return (*zip(inner_parts, inner_weight), (gate_low, gate_weight))


def ffn_backward(stored, low_grad, weights):
    gate_weight, up_weight, down_weight = weights
    normed, gate, up, hidden = stored
    hidden_grad = mm(low_grad, down_weight)
    sig = jax.nn.sigmoid(gate)
    gate_low = (hidden_grad * up * sig * (1.0 + gate * (1.0 - sig))).astype(BF)
    up_low = (hidden_grad * gate * sig).astype(BF)
    return [(gate_low, gate_weight), (up_low, up_weight)]


def shards(
    layout,
    layer_input,
    upstream,
    norm_gains,
    mixer_input,
    conv_taps,
    conv_bias,
    mixer_select,
    mixer_step,
    step_bias,
    decay_log,
    skip_gain,
    mixer_output,
    first_gate_up,
    first_down,
    attention_input,
    attention_output,
    second_gate_up,
    second_down,
):
    mine = lambda v: half_of(v, "b")
    theirs = lambda v: half_of(v, "b", True)
    place = jnp.stack([bit("x"), bit("c")]).astype(jnp.int32)
    quarter = place[0] * 2 + place[1]
    rows = layer_input.shape[0] // QUARTERS
    tokens = 8 * rows
    own_rows = lambda v: layout.columns_in(lax.dynamic_slice_in_dim(v, quarter * rows, rows, axis=0))
    blocks = lambda v: v.reshape(2, 2, 2, rows, v.shape[-1])

    pump, weights, grads = Pump(layout), {}, {}

    def swapped(arrays, *tokens):
        with jax.named_scope("pack"):
            if tokens:
                arrays = lax.optimization_barrier((tuple(arrays),) + tokens)[0]
            flat = lambda v: v.reshape(v.shape[0], -1)
            kept = jnp.concatenate([flat(mine(a)) for a in arrays], axis=1)
            return kept, exchange(jnp.concatenate([flat(theirs(a)) for a in arrays], axis=1), "b")

    def request(names, arrays, *tokens):
        kept, got = swapped(arrays, *tokens)
        width = kept.shape[1] // len(names)
        for at, name in enumerate(names):
            cut = slice(at * width, (at + 1) * width)
            pump.add(fetch_job(layout, kept[:, cut], got[:, cut], weights, name))
        return got

    here, _, wide = attention_input.shape
    width = wide // 2
    stream0 = own_rows(layer_input).astype(F32)
    gains = layout.columns_in(norm_gains)
    upstream_rows = own_rows(upstream)
    with jax.named_scope("inner_fetch"):
        first = request(["inner0", "inner1"], [mixer_input[:, 0]])
        pump.flush()
    normed0 = gather_rows(tied(rms(stream0, gains[0]), first))
    request(["small"], [jnp.concatenate([mixer_step, mixer_select], axis=0)], normed0)
    pump.flush()
    second = request(["gate", "out"], [mixer_input[:, 1], mixer_output], first)
    third = request(
        ["gate1", "up1", "down1"], [first_gate_up, first_down], normed0, second,
    )
    normed0 = pump.turn(normed0, 1)
    channel = tuple(mine(v) for v in (conv_taps, conv_bias, step_bias, decay_log, skip_gain))
    inner = jnp.concatenate([mm(normed0, weights["inner0"]), mm(normed0, weights["inner1"])], axis=1)
    inner = pump.turn(inner, 1)
    low4 = gather_rows(tied(upstream_rows, inner))
    inner = in_time(blocks(inner))
    conv_out = jax.nn.silu(conv_total(inner, channel[0], channel[1])).astype(BF)
    select_rows, step_rows = mixer_select.shape[0], mixer_step.shape[0]
    both = layout.columns_out(weights["small"], 0).reshape(-1, select_rows + step_rows, conv_out.shape[-1])
    select_weight = both[:, step_rows:].reshape(-1, conv_out.shape[-1])
    step_weight = both[:, :step_rows].reshape(-1, conv_out.shape[-1])
    partial = mm_nt(conv_out.reshape(tokens, -1), select_weight)
    with jax.named_scope("select_total"):
        selected = channel_total(partial, True)
    selected = pump.turn(selected)
    request(["query_key", "value_out"], [attention_input, attention_output], inner, third)
    rank, states_n = step_weight.shape[0], decay_log.shape[0]
    step_low = selected[:, :rank].astype(BF)
    raw = mm(step_low, step_weight).reshape(conv_out.shape)
    sel = selected[:, rank:].reshape(2, tokens // 2 // ROWS, ROWS, -1).transpose(0, 1, 3, 2)
    raw = pump.until(raw, weights, "gate")
    gate = blocks(mm(normed0, weights["gate"]))
    mixed, gated, hist = scan_forward(conv_out.astype(F32), raw, gate, sel, *channel[2:], place)
    gated = gated.reshape(tokens, -1).astype(BF)
    gated = pump.until(gated, weights, "out")
    mixer_stored = (normed0, inner, gate, conv_out, step_low, raw, sel, mixed, gated, hist)
    mixer_weights = ((weights["inner0"], weights["inner1"]), weights["gate"], weights["out"], select_weight, step_weight)
    stream1 = tied(pump.turn(stream0 + scatter_rows([(gated, weights["out"])])), low4)
    request(
        ["gate2", "up2", "down2"], [second_gate_up, second_down], gated
    )

    def ffn(normed, tag):
        normed = pump.until(normed, weights, "gate" + tag, "up" + tag)
        gate, up = mm(normed, weights["gate" + tag]), mm(normed, weights["up" + tag])
        hidden = (jax.nn.silu(gate) * up).astype(BF)
        return hidden, (normed, gate, up, hidden)

    hidden1, first_stored = ffn(pump.turn(gather_rows(rms(stream1, gains[1]))), "1")
    hidden1 = pump.until(hidden1, weights, "down1")
    first_weights = tuple(weights[n] for n in ("gate1", "up1", "down1"))
    stream2 = pump.turn(stream1 + scatter_rows([(hidden1, weights["down1"])]))

    normed2 = pump.turn(gather_rows(rms(stream2, gains[2])))
    normed2 = pump.until(normed2, weights, "query_key", "value_out")
    value_weight, out_weight = weights["value_out"][:, :width], weights["value_out"][:, width:]
    triple = jnp.concatenate([mm(normed2, weights["query_key"]), mm(normed2, value_weight)], axis=1)
    order = (jnp.arange(2)[None, :] ^ place[0]) * 2 + (jnp.arange(2)[:, None] ^ place[1])
    tables = rotary_tables((order[:, :, None] * rows + jnp.arange(rows)).reshape(-1))
    turned, context = attention_call(
        attention_forward_kernel, "attention_forward", [blocks(triple)], (3 * width, width), tables
    )
    context = context.reshape(tokens, -1)
    stream3 = pump.turn(stream2 + scatter_rows([(context, out_weight)]))

    hidden3, second_stored = ffn(gather_rows(rms(stream3, gains[3])), "2")
    hidden3 = pump.until(hidden3, weights, "down2")
    second_weights = tuple(weights[n] for n in ("gate2", "up2", "down2"))

    pump.add(settle_job(layout, low4, hidden3, grads, "down2"))
    pump.begin(hidden3, 1)
    products = ffn_backward(second_stored, low4, second_weights)
    normed3 = second_stored[0]
    for name, (right, _) in zip(("gate2", "up2"), products):
        pump.add(settle_job(layout, normed3, right, grads, name))
    back, gain3 = rms_back(stream3, gains[3], pump.turn(scatter_rows(products)))
    grad3 = upstream_rows.astype(F32) + back
    stream4 = stream3 + scatter_rows([(hidden3, weights["down2"])])

    low3 = gather_rows(grad3.astype(BF))
    pump.add(settle_job(layout, low3, context, grads, "attention_out"))
    low3 = pump.turn(low3, 2)
    context_grad = mm(low3, out_weight).astype(BF)
    (triple_low,) = attention_call(
        attention_backward_kernel, "attention_backward", [turned, blocks(context_grad)], (3 * width,), tables
    )
    triple_low = triple_low.reshape(tokens, -1)
    pump.add(settle_job(layout, normed2, triple_low, grads, "attention_in"))
    back, gain2 = rms_back(
        stream2,
        gains[2],
        pump.turn(
            scatter_rows([(triple_low[:, : 2 * width], weights["query_key"]), (triple_low[:, 2 * width :], value_weight)])
        ),
    )
    grad2 = grad3 + back
    low2 = pump.turn(gather_rows(grad2.astype(BF)), 0)
    products = ffn_backward(first_stored, low2, first_weights)
    pump.add(settle_job(layout, low2, first_stored[3], grads, "down1"))
    pump.begin(low2, 1)
    for name, (right, _) in zip(("gate1", "up1"), products):
        pump.add(settle_job(layout, first_stored[0], right, grads, name))
    back, gain1 = rms_back(stream1, gains[1], pump.turn(scatter_rows(products), 2))
    grad1 = grad2 + back

    low1 = gather_rows(grad1.astype(BF))
    pump.add(settle_job(layout, low1, mixer_stored[8], grads, "out"))
    low1 = pump.turn(low1, 1, 1)
    products = mixer_backward(mixer_stored, low1, mixer_weights, channel, place, pump, grads)
    scattered = pump.turn(scatter_rows(products), 0)
    back, gain0 = rms_back(stream0, gains[0], scattered)
    with jax.named_scope("gain_sums"):
        gains_grad = layout.columns_out(jnp.stack([gain0, gain1, gain2, gain3]))
        for axis in ("c", "x", "b") + layout.sums:
            gains_grad = gains_grad + exchange(gains_grad, axis)
    gains_grad = pump.turn(gains_grad, 0)
    pump.flush()
    small = grads["small"]
    with jax.named_scope("last_gather"):
        input_grad = gather_sequence(layout.columns_out((grad1 + back).astype(BF))).astype(F32)
        layer_output = gather_sequence(layout.columns_out(stream4.astype(BF)))

    dp_index = lax.axis_index(layout.high + ("b", "y"))
    select_all, step_all = select_weight.shape[0], step_weight.shape[0]
    select_grad = lax.dynamic_slice_in_dim(small[:select_all], dp_index * select_rows, select_rows, axis=0)
    step_grad = lax.dynamic_slice_in_dim(
        small[select_all : select_all + step_all], dp_index * step_rows, step_rows, axis=0
    )
    rest = small[select_all + step_all :]
    count = conv_taps.shape[0]
    taps_grad, conv_bias_grad, step_bias_grad = rest[:count], rest[count], rest[count + 1]
    decay_grad, skip_grad = rest[count + 2 : count + 2 + states_n], rest[count + 2 + states_n]

    matrix = lambda halves: jnp.concatenate(halves, axis=1).astype(F32)
    pair = lambda low, high: jnp.stack([jnp.concatenate(low, axis=1), jnp.concatenate(high, axis=1)], axis=1).astype(F32)
    parts = lambda halves, count: jnp.stack([h.reshape(here, count, -1) for h in halves], axis=2).astype(F32)
    return (
        layer_output,
        input_grad,
        gains_grad,
        pair([jnp.concatenate(h, axis=1) for h in zip(grads["inner0"], grads["inner1"])], grads["gate"]),
        taps_grad,
        conv_bias_grad,
        select_grad,
        step_grad,
        step_bias_grad,
        decay_grad,
        skip_grad,
        matrix(grads["out"]),
        pair(grads["gate1"], grads["up1"]),
        matrix(grads["down1"]),
        parts(grads["attention_in"], 3).reshape(here, 3, -1),
        matrix(grads["attention_out"]),
        pair(grads["gate2"], grads["up2"]),
        matrix(grads["down2"]),
    )


def solution(mesh):
    n_dp, n_tensor = mesh.devices.shape
    bits = n_dp.bit_length() - 1
    assert n_dp == 1 << bits and bits >= 2 and n_tensor == 4
    high = tuple("a%d" % k for k in range(bits - 2))
    names = high + ("b", "y", "x", "c")
    cube = jax.sharding.Mesh(mesh.devices.reshape((2,) * len(names)), names)
    dp, tensor = high + ("b", "y"), ("x", "c")
    row, both, col = P(dp, None), P(dp, tensor), P(None, tensor)
    three, vec = P(dp, None, tensor), P(tensor)
    return jax.shard_map(
        functools.partial(shards, Layout(high)),
        mesh=cube,
        in_specs=(
            row, row, P(), three, col, vec, both, both, vec, col, vec, both, three, both, three, both, three, both,
        ),
        out_specs=(
            row, row, P(), three, col, vec, both, both, vec, col, vec, both, three, both, three, both, three, both,
        ),
        check_vma=False,
    )
```

```python
import functools
import jax
import jax.numpy as jnp
from jax import lax
from jax.experimental import pallas as pl
from jax.experimental.pallas import tpu as pltpu
from jax.sharding import PartitionSpec as P

HEAD_DIM = 64
WINDOW = 2048
EPS = 1e-05
ROPE_BASE = 10000.0
MASKED = -1e30
BF = jnp.bfloat16
F32 = jnp.float32
SWAP = ((0, 1), (1, 0))
QUARTERS = 4
LANES = 128
ROWS = 8


def scan_forward_kernel(
    place_ref, x_ref, raw_ref, gate_ref, sel_ref, bias_ref, decay_ref, skip_ref, y_ref, gated_ref, hist_ref, state_ref
):
    seqs, steps, channels = x_ref.shape
    blocks = channels // LANES
    states_n = decay_ref.shape[0]
    pairs = [(s, j) for s in range(seqs) for j in range(blocks)]

    @pl.when(pl.program_id(1) == 0)
    def _():
        state_ref[...] = jnp.zeros_like(state_ref)

    def lanes(j):
        return slice(j * LANES, (j + 1) * LANES)

    rates = [-jnp.exp(decay_ref[:, lanes(j)]) for j in range(blocks)]

    def chunk(k, states):
        states = list(states)
        rows = pl.ds(pl.multiple_of(k * ROWS, ROWS), ROWS)
        x_t, d_t, dx_t = {}, {}, {}
        for s, j in pairs:
            x_t[s, j] = x_ref[s, rows, lanes(j)]
            d_t[s, j] = jax.nn.softplus(raw_ref[s, rows, lanes(j)] + bias_ref[:, lanes(j)])
            dx_t[s, j] = d_t[s, j] * x_t[s, j]
        outs = {p: [] for p in pairs}
        for i in range(ROWS):
            for s in range(seqs):
                sel_b = jnp.broadcast_to(sel_ref[s, k, :states_n, i : i + 1], (states_n, LANES))
                sel_c = jnp.broadcast_to(sel_ref[s, k, states_n:, i : i + 1], (states_n, LANES))
                for j in range(blocks):
                    at = s * blocks + j
                    before = states[at]
                    hist_ref[s, k * ROWS + i, :, lanes(j)] = before
                    factor = jnp.exp(d_t[s, j][i : i + 1] * rates[j])
                    after = factor * before + dx_t[s, j][i : i + 1] * sel_b
                    states[at] = after
                    outs[s, j].append(jnp.sum(after * sel_c, axis=0, keepdims=True))
        for s, j in pairs:
            y = jnp.concatenate(outs[s, j], axis=0) + skip_ref[:, lanes(j)] * x_t[s, j]
            gate = gate_ref[0, s, 0, rows, lanes(j)]
            y_ref[s, rows, lanes(j)] = y
            gated_ref[0, s, 0, rows, lanes(j)] = y * gate * jax.nn.sigmoid(gate)
        return tuple(states)

    first = tuple(state_ref[s * blocks + j] for s, j in pairs)
    last = lax.fori_loop(0, steps // ROWS, chunk, first)
    for at, value in enumerate(last):
        state_ref[at] = value


def group_sums(states_n):
    shape = (ROWS, ROWS * states_n)
    step = lax.broadcasted_iota(jnp.int32, shape, 1) // states_n
    return (step == lax.broadcasted_iota(jnp.int32, shape, 0)).astype(jnp.bfloat16)


def scan_backward_kernel(
    place_ref, x_ref, raw_ref, gate_ref, y_ref, grad_ref, hist_ref, sel_ref, bias_ref, decay_ref, skip_ref,
    dgate_ref, dx_ref, draw_ref, dsel_ref, ddecay_ref, dskip_ref, dbias_ref,
    adj_ref, step_ref, drive_ref, out_ref, first_ref, second_ref, db_ref, dc_ref,
):
    _, steps, channels = x_ref.shape
    blocks = channels // LANES
    states_n = decay_ref.shape[0]

    @pl.when(pl.program_id(1) == 0)
    def _():
        adj_ref[...] = jnp.zeros_like(adj_ref)

    @pl.when((pl.program_id(0) == 0) & (pl.program_id(1) == 0))
    def _():
        ddecay_ref[...] = jnp.zeros_like(ddecay_ref)
        dskip_ref[...] = jnp.zeros_like(dskip_ref)
        dbias_ref[...] = jnp.zeros_like(dbias_ref)

    def lanes(j):
        return slice(j * LANES, (j + 1) * LANES)

    rates = [-jnp.exp(decay_ref[:, lanes(j)]) for j in range(blocks)]
    sums = group_sums(states_n)
    ones = jnp.ones((ROWS, LANES), jnp.bfloat16)
    over_lanes = lambda v: lax.dot_general(ones, v, (((1,), (1,)), ((), ())), preferred_element_type=jnp.float32)

    def chunk(step, carry):
        adjoint, decay_sum = list(carry[0]), list(carry[1])
        k = steps // ROWS - 1 - step
        rows = pl.ds(pl.multiple_of(k * ROWS, ROWS), ROWS)
        x = x_ref[0, rows, :]
        z = raw_ref[0, rows, :] + bias_ref[...]
        delta = jax.nn.softplus(z)
        gate = gate_ref[0, 0, 0, rows, :]
        sig = jax.nn.sigmoid(gate)
        grad = grad_ref[0, 0, 0, rows, :]
        dy = grad * gate * sig
        dgate_ref[0, 0, 0, rows, :] = grad * y_ref[0, rows, :] * sig * (1.0 + gate * (1.0 - sig))
        step_ref[...] = delta
        drive_ref[...] = delta * x
        out_ref[...] = dy
        for i in reversed(range(ROWS)):
            place = slice(i * states_n, (i + 1) * states_n)
            sel_b = jnp.broadcast_to(sel_ref[0, k, :states_n, i : i + 1], (states_n, LANES))
            sel_c = jnp.broadcast_to(sel_ref[0, k, states_n:, i : i + 1], (states_n, LANES))
            db = jnp.zeros((states_n, LANES), jnp.float32)
            dc = jnp.zeros((states_n, LANES), jnp.float32)
            for j in range(blocks):
                before = hist_ref[0, k * ROWS + i, :, lanes(j)]
                width = step_ref[i : i + 1, lanes(j)]
                drive = drive_ref[i : i + 1, lanes(j)]
                out = out_ref[i : i + 1, lanes(j)]
                factor = jnp.exp(width * rates[j])
                after = factor * before + drive * sel_b
                lam = adjoint[j] + out * sel_c
                dc = dc + out * after
                db = db + drive * lam
                first_ref[place, lanes(j)] = (lam * sel_b).astype(jnp.bfloat16)
                back = lam * factor
                adjoint[j] = back
                through = back * before
                second_ref[place, lanes(j)] = (rates[j] * through).astype(jnp.bfloat16)
                decay_sum[j] = decay_sum[j] + width * through
            db_ref[place, :] = db.astype(jnp.bfloat16)
            dc_ref[place, :] = dc.astype(jnp.bfloat16)
        dsel_ref[0, k, 0:ROWS, :] = over_lanes(db_ref[...])
        dsel_ref[0, k, ROWS : 2 * ROWS, :] = over_lanes(dc_ref[...])
        one = jnp.dot(sums, first_ref[...], preferred_element_type=jnp.float32)
        two = jnp.dot(sums, second_ref[...], preferred_element_type=jnp.float32)
        dx_ref[0, rows, :] = dy * skip_ref[...] + delta * one
        draw = (two + x * one) * jax.nn.sigmoid(z)
        draw_ref[0, rows, :] = draw
        dskip_ref[...] += dy * x
        dbias_ref[...] += draw
        return tuple(adjoint), tuple(decay_sum)

    carry = (
        tuple(adj_ref[j] for j in range(blocks)),
        tuple(jnp.zeros((states_n, LANES), jnp.float32) for _ in range(blocks)),
    )
    adjoint, decay_sum = lax.fori_loop(0, steps // ROWS, chunk, carry, unroll=4)
    for j in range(blocks):
        adj_ref[j] = adjoint[j]
        ddecay_ref[:, lanes(j)] += rates[j] * decay_sum[j]


def quarter_block(place, quarter):
    return place[1] ^ (quarter & 1), place[0] ^ (quarter >> 1)


def scan_call(kernel, name, ins, outs, sel, vectors, place, reverse, extra_outs=(), scratch=()):
    seqs, length, channels = ins[0][1].shape
    states_n = vectors[1].shape[0]
    steps = length // QUARTERS
    turn = lambda i: QUARTERS - 1 - i if reverse else i

    def spec(kind, width):
        if kind == "time":
            return pl.BlockSpec((1, steps, width), lambda s, i, place: (s, turn(i), 0))
        if kind == "hist":
            return pl.BlockSpec((1, steps, states_n, width), lambda s, i, place: (s, turn(i), 0, 0))
        if kind == "dsel":
            return pl.BlockSpec((1, steps // ROWS, 2 * ROWS, ROWS * states_n), lambda s, i, place: (s, turn(i), 0, 0))
        if kind == "sel":
            return pl.BlockSpec((1, steps // ROWS, 2 * states_n, ROWS), lambda s, i, place: (s, turn(i), 0, 0))
        return pl.BlockSpec(
            (1, 1, 1, steps, width),
            lambda s, i, place: (quarter_block(place, turn(i))[0], s, quarter_block(place, turn(i))[1], 0, 0),
        )

    whole = lambda shape: pl.BlockSpec(shape, lambda s, i, place: (0,) * len(shape))
    shape_of = {
        "time": (seqs, length, channels),
        "hist": (seqs, length, states_n, channels),
        "dsel": sel.shape[:2] + (2 * ROWS, ROWS * states_n),
        "mine": (2, seqs, 2, steps, channels),
    }
    elems = seqs * length * channels * states_n
    full = lambda shape: jax.ShapeDtypeStruct(shape, jnp.float32)
    return pl.pallas_call(
        kernel,
        grid_spec=pltpu.PrefetchScalarGridSpec(
            num_scalar_prefetch=1,
            grid=(seqs, QUARTERS),
            in_specs=[spec(kind, channels) for kind, _ in ins] + [spec("sel", 0)] + [whole(v.shape) for v in vectors],
            out_specs=[spec(kind, channels) for kind in outs] + [whole(shape) for shape in extra_outs],
            scratch_shapes=[pltpu.VMEM((channels // LANES, states_n, LANES), jnp.float32)] + list(scratch),
        ),
        out_shape=[full(shape_of[kind]) for kind in outs] + [full(shape) for shape in extra_outs],
        cost_estimate=pl.CostEstimate(
            flops=(60 if reverse else 20) * elems, bytes_accessed=4 * elems, transcendentals=elems
        ),
        compiler_params=pltpu.CompilerParams(vmem_limit_bytes=48 * 1024 * 1024),
        name=name,
    )(place, *[v for _, v in ins], sel, *vectors)


def scan_forward(x, raw, gate, sel, bias, decay, skip, place):
    ins = (("time", x), ("time", raw), ("mine", gate))
    vectors = (bias.reshape(1, -1), decay, skip.reshape(1, -1))
    return scan_call(scan_forward_kernel, "scan_forward", ins, ("time", "mine", "hist"), sel, vectors, place, False)


def scan_backward(x, raw, gate, y, grad, hist, sel, bias, decay, skip, place):
    ins = (("time", x), ("time", raw), ("mine", gate), ("time", y), ("mine", grad), ("hist", hist))
    vectors = (bias.reshape(1, -1), decay, skip.reshape(1, -1))
    extra = (decay.shape, (ROWS, x.shape[2]), (ROWS, x.shape[2]))
    group, channels = ROWS * decay.shape[0], x.shape[2]
    scratch = (
        [pltpu.VMEM((ROWS, channels), jnp.float32)] * 3
        + [pltpu.VMEM((group, channels), jnp.bfloat16)] * 2
        + [pltpu.VMEM((group, LANES), jnp.bfloat16)] * 2
    )
    outs = ("mine", "time", "time", "dsel")
    return scan_call(scan_backward_kernel, "scan_backward", ins, outs, sel, vectors, place, True, extra, scratch)


def turn_heads(value, cosine, sine):
    size = value.shape[1]
    half = HEAD_DIM // 2
    lane = lax.broadcasted_iota(jnp.int32, value.shape, 1)
    partner = jnp.where(lane % HEAD_DIM < half, pltpu.roll(value, size - half, 1), pltpu.roll(value, half, 1))
    return value * cosine + partner * sine


def head_pair(ref, part, pair, pairs):
    at = (part * pairs + pair) * LANES
    return ref[:, 0, :, :, at : at + LANES].reshape(-1, LANES)


def pair_weights(queries, keys, head_lanes, mask):
    zero = jnp.zeros_like(queries)
    scores = lax.dot_general(
        jnp.where(head_lanes, queries, zero), keys, (((1,), (1,)), ((), ())), preferred_element_type=jnp.float32
    )
    scores = jnp.where(mask, scores * HEAD_DIM**-0.5, MASKED)
    raised = jnp.exp(scores - jnp.max(scores, axis=1, keepdims=True))
    return raised / jnp.sum(raised, axis=1, keepdims=True)


def attention_forward_kernel(triple_ref, cos_ref, sin_ref, row_ref, col_ref, turned_ref, context_ref):
    pairs = context_ref.shape[-1] // LANES
    shape = context_ref.shape[:-1] + (LANES,)
    mask = (col_ref[...] <= row_ref[...]) & (row_ref[...] - col_ref[...] < WINDOW)
    cosine, sine = cos_ref[...], sin_ref[...]
    low_lanes = lax.broadcasted_iota(jnp.int32, (1, LANES), 1) < HEAD_DIM
    for pair in range(pairs):
        queries = turn_heads(head_pair(triple_ref, 0, pair, pairs), cosine, sine).astype(jnp.bfloat16)
        keys = turn_heads(head_pair(triple_ref, 1, pair, pairs), cosine, sine).astype(jnp.bfloat16)
        values = head_pair(triple_ref, 2, pair, pairs).astype(jnp.bfloat16)
        outs = []
        for head in range(LANES // HEAD_DIM):
            lanes = low_lanes if head == 0 else ~low_lanes
            attend = pair_weights(queries, keys, lanes, mask).astype(jnp.bfloat16)
            outs.append(jnp.dot(attend, values, preferred_element_type=jnp.float32))
        context = jnp.where(low_lanes, outs[0], outs[1]).astype(jnp.bfloat16)
        context_ref[..., pair * LANES : (pair + 1) * LANES] = context.reshape(shape)
        for part, value in enumerate((queries, keys, values)):
            at = (part * pairs + pair) * LANES
            turned_ref[..., at : at + LANES] = value.reshape(shape)


def attention_backward_kernel(turned_ref, grad_ref, cos_ref, sin_ref, row_ref, col_ref, out_ref):
    pairs = grad_ref.shape[-1] // LANES
    shape = grad_ref.shape[:-1] + (LANES,)
    mask = (col_ref[...] <= row_ref[...]) & (row_ref[...] - col_ref[...] < WINDOW)
    cosine, sine = cos_ref[...], -sin_ref[...]
    low_lanes = lax.broadcasted_iota(jnp.int32, (1, LANES), 1) < HEAD_DIM
    dot = lambda a, b, dims: lax.dot_general(a, b, (dims, ((), ())), preferred_element_type=jnp.float32)
    for pair in range(pairs):
        queries, keys, values = (head_pair(turned_ref, part, pair, pairs) for part in range(3))
        grads = head_pair(grad_ref, 0, pair, pairs)
        parts = [[], [], []]
        for head in range(LANES // HEAD_DIM):
            lanes = low_lanes if head == 0 else ~low_lanes
            full = pair_weights(queries, keys, lanes, mask)
            attend = full.astype(jnp.bfloat16)
            own = jnp.where(lanes, grads, jnp.zeros_like(grads))
            weight_grad = dot(own, values, ((1,), (1,)))
            delta = jnp.sum(full * weight_grad, axis=1, keepdims=True)
            score_grad = (full * (weight_grad - delta)).astype(jnp.bfloat16)
            parts[0].append(dot(score_grad, keys, ((1,), (0,))) * HEAD_DIM**-0.5)
            parts[1].append(dot(score_grad, queries, ((0,), (0,))) * HEAD_DIM**-0.5)
            parts[2].append(dot(attend, grads, ((0,), (0,))))
        for part, (low, high) in enumerate(parts):
            value = jnp.where(low_lanes, low, high)
            if part < 2:
                value = turn_heads(value, cosine, sine)
            at = (part * pairs + pair) * LANES
            out_ref[..., at : at + LANES] = value.astype(jnp.bfloat16).reshape(shape)


def rotary_tables(positions):
    half = HEAD_DIM // 2
    frequency = ROPE_BASE ** (-jnp.arange(half, dtype=F32) * 2.0 / HEAD_DIM)
    angles = positions.astype(F32)[:, None] * frequency[None, :]
    cosine, sine = jnp.cos(angles), jnp.sin(angles)
    twice = lambda low, high: jnp.concatenate([low, high] * (LANES // HEAD_DIM), axis=1)
    return twice(cosine, cosine), twice(-sine, sine), positions[:, None], positions[None, :]


def attention_call(kernel, name, ins, widths, tables):
    lead = ins[0].shape[:-1]
    split = lambda width: pl.BlockSpec((lead[0], 1) + lead[2:] + (width,), lambda s: (0, s, 0, 0, 0))
    whole = lambda a: pl.BlockSpec(a.shape, lambda s: (0, 0))
    length = lead[0] * lead[2] * lead[3]
    heads = widths[-1] // HEAD_DIM
    flops = 2 * lead[1] * 2 * length * length * LANES * 5 * max(heads, 1)
    return pl.pallas_call(
        kernel,
        grid=(lead[1],),
        in_specs=[split(a.shape[-1]) for a in ins] + [whole(t) for t in tables],
        out_specs=[split(w) for w in widths],
        out_shape=[jax.ShapeDtypeStruct(lead + (w,), jnp.bfloat16) for w in widths],
        cost_estimate=pl.CostEstimate(flops=flops, bytes_accessed=4 * 1024 * 1024, transcendentals=length * length * 8),
        compiler_params=pltpu.CompilerParams(vmem_limit_bytes=32 * 1024 * 1024),
        name=name,
    )(*ins, *tables)


def bit(axis):
    return lax.axis_index(axis)


def exchange(value, axis):
    return lax.ppermute(value, axis, SWAP)


def exchange_diagonal(value):
    return lax.ppermute(value, ("b", "x"), ((0, 3), (1, 2), (2, 1), (3, 0)))


def ordered(axis, mine, other):
    first = bit(axis) == 0
    return lax.select(first, mine, other), lax.select(first, other, mine)


def half_of(value, axis, other=False):
    width = value.shape[-1] // 2
    at = bit(axis) if not other else 1 - bit(axis)
    return lax.dynamic_slice_in_dim(value, at * width, width, axis=value.ndim - 1)


def tied(value, *tokens):
    return lax.optimization_barrier((value,) + tokens)[0]


class Pump:
    def __init__(self, layout):
        self.layout, self.waiting, self.flying = layout, [], []

    def add(self, job):
        self.waiting.append(job)

    def land(self, token):
        token, flying = lax.optimization_barrier((token, [results for _, results in self.flying]))
        self.flying = [(job, results) for (job, _), results in zip(self.flying, flying)]
        return token

    def turn(self, token, count=1, hold=0):
        split = len(self.flying) - hold
        going, held = self.flying[:split], self.flying[split:]
        if going:
            flat = [r for _, results in going for r in results]
            tied_all = lax.optimization_barrier((token, *flat))
            token, flat = tied_all[0], list(tied_all[1:])
        asks = []
        for job, results in going:
            got, flat = flat[: len(results)], flat[len(results) :]
            try:
                asks.append((job, job.send(got)))
            except StopIteration:
                pass
        for job in self.waiting[:count]:
            asks.append((job, [(tied(v, token), axis) for v, axis in next(job)]))
        del self.waiting[:count]
        self.flying = held + [(job, [exchange(v, axis) for v, axis in ask]) for job, ask in asks]
        return token

    def begin(self, token, count=1):
        for job in self.waiting[:count]:
            self.flying.append((job, [exchange(tied(v, token), axis) for v, axis in next(job)]))
        del self.waiting[:count]

    def until(self, token, store, *names):
        while not all(name in store for name in names):
            token = self.turn(token)
        return token

    def flush(self):
        jobs = [(job, [exchange(v, axis) for v, axis in next(job)]) for job in self.waiting]
        for job, results in self.flying + jobs:
            try:
                while True:
                    results = [exchange(v, axis) for v, axis in job.send(list(results))]
            except StopIteration:
                pass
        self.waiting, self.flying = [], []


class Layout:
    def __init__(self, high):
        self.high = high
        self.sums = high + ("y",)

    def split_bits(self, value, at):
        k = len(self.high) + 2
        return value.reshape(value.shape[:at] + (2,) * k + (value.shape[at] >> k,) + value.shape[at + 1 :])

    def turned(self, value, at):
        for place, axis in enumerate(self.high + ("b", "y")):
            if axis != "b":
                value = lax.select(bit(axis) == 0, value, lax.rev(value, (at + place,)))
        return value

    def columns_in(self, value, at=-1):
        shape, at = value.shape, at % value.ndim
        value = self.turned(self.split_bits(value, at), at)
        return jnp.moveaxis(value, at + len(self.high) + 1, at).reshape(shape)

    def columns_out(self, value, at=-1):
        shape, at = value.shape, at % value.ndim
        value = jnp.moveaxis(self.split_bits(value, at), at, at + len(self.high) + 1)
        return self.turned(value, at).reshape(shape)


def fetch_job(layout, mine, other, store, name):
    own = jnp.concatenate(ordered("b", mine, other), axis=0)
    axes = layout.high[::-1]
    if len(axes) == 1:
        high, beside = yield [(own, axes[0]), (own, "y")]
        (far,) = yield [(high, "y")]
        pieces = [own, high, beside, far]
    else:
        pieces = [own]
        for axis in axes + ("y",):
            got = yield [(piece, axis) for piece in pieces]
            pieces = pieces + list(got)
    store[name] = jnp.concatenate(pieces, axis=0)


def settle_job(layout, left, right, store, name):
    width = left.shape[1]
    got = []
    product = lambda lo, hi: sum((g[lo:hi].astype(F32) for g in got), mm_tn(left[:, lo:hi], right))
    for axis in ("y",) + layout.high:
        width = width // 2
        got += yield [(product(width, 2 * width).astype(BF), axis)]
    total = product(0, width).astype(BF)
    keep, send = ordered("b", total[: width // 2], total[width // 2 :])
    (other,) = yield [(send, "b")]
    store[name] = ordered("b", keep, other)


def small_job(layout, value, store, name):
    for axis in layout.sums:
        (got,) = yield [(value.astype(BF), axis)]
        value = value + got.astype(F32)
    (got,) = yield [(value.astype(BF), "b")]
    store[name] = jnp.concatenate(ordered("b", value, got.astype(F32)), axis=1)


def gather_rows(rows):
    with jax.named_scope("rows_gather"):
        beside = exchange(rows, "x")
        across = exchange(rows, "b")
        corner = exchange_diagonal(rows)
        mine = jnp.concatenate([rows, beside, across, corner], axis=-2)
        return jnp.concatenate([mine, exchange(mine, "c")], axis=-2)


def scatter_rows(products):
    with jax.named_scope("rows_scatter"):
        half = products[0][0].shape[0] // 2
        send = sum(mm_nt(v[half:], w) for v, w in products).astype(BF)
        got = exchange(send, "c")
        keep = sum(mm_nt(v[:half], w) for v, w in products) + got.astype(F32)
        rows = half // 4
        low = keep[rows:].astype(BF)
        beside = exchange(low[:rows], "x")
        across = exchange(low[rows : 2 * rows], "b")
        corner = exchange_diagonal(low[2 * rows :])
        return keep[:rows] + beside.astype(F32) + across.astype(F32) + corner.astype(F32)


def in_time(value):
    left, right = ordered("x", value[:, :, 0], value[:, :, 1])
    halves = [jnp.stack(ordered("c", half[0], half[1]), axis=1) for half in (left, right)]
    return jnp.stack(halves, axis=1).reshape(value.shape[1], -1, value.shape[-1])


def from_time(value, rows):
    value = value.reshape(value.shape[0], 2, 2, rows, value.shape[-1])
    parts = [jnp.stack(ordered("x", v[:, 0], v[:, 1]), axis=1) for v in ordered("c", value[:, :, 0], value[:, :, 1])]
    return jnp.stack(parts)


def gather_sequence(rows):
    even, odd = ordered("c", rows, exchange(rows, "c"))
    pair = jnp.stack([even, odd])
    left, right = ordered("x", pair, exchange(pair, "x"))
    return jnp.stack([left, right]).reshape(QUARTERS * rows.shape[0], -1)


def channel_total(partial, low=False):
    narrow = (lambda v: v.astype(BF)) if low else (lambda v: v)
    total = partial + exchange(narrow(partial), "c").astype(F32)
    return chip_total(total, narrow)


def chip_total(total, narrow=lambda v: v.astype(BF)):
    total = total + exchange(narrow(total), "x").astype(F32)
    other = exchange(narrow(total), "b").astype(F32)
    rows = total.shape[0] // 2
    return total + jnp.concatenate([other[rows:], other[:rows]], axis=0)


def rms(stream, gain_row):
    scale = lax.rsqrt(jnp.mean(stream * stream, axis=-1, keepdims=True) + EPS)
    return (stream * scale * gain_row[None, :]).astype(BF)


def rms_back(stream, gain_row, grad):
    scale = lax.rsqrt(jnp.mean(stream * stream, axis=-1, keepdims=True) + EPS)
    gain_grad = jnp.sum(grad * stream * scale, axis=0)
    scaled = grad * gain_row[None, :]
    inner = jnp.mean(scaled * stream, axis=-1, keepdims=True)
    return scale * scaled - stream * (scale * scale * scale * inner), gain_grad


def mm(left, right):
    return jnp.dot(left, right, preferred_element_type=F32)


def mm_nt(left, right):
    return lax.dot_general(left, right, (((1,), (1,)), ((), ())), preferred_element_type=F32)


def mm_tn(left, right):
    return lax.dot_general(left, right, (((0,), (0,)), ((), ())), preferred_element_type=F32)


def conv_total(inner, taps, bias):
    count, length = taps.shape[0], inner.shape[1]
    padded = jnp.pad(inner, ((0, 0), (count - 1, 0), (0, 0)))
    total = bias[None, None, :]
    for k in range(count):
        total = total + taps[k][None, None, :] * padded[:, k : k + length]
    return total


def conv_back(grad, inner, taps):
    count, length = taps.shape[0], inner.shape[1]
    before = jnp.pad(inner, ((0, 0), (count - 1, 0), (0, 0)))
    after = jnp.pad(grad, ((0, 0), (0, count - 1), (0, 0)))
    inner_grad = 0.0
    taps_grad = []
    for k in range(count):
        shift = count - 1 - k
        inner_grad = inner_grad + taps[k][None, None, :] * after[:, shift : shift + length]
        taps_grad.append(jnp.sum(grad * before[:, k : k + length], axis=(0, 1)))
    return inner_grad, jnp.stack(taps_grad), jnp.sum(grad, axis=(0, 1))


def mixer_backward(stored, low_grad, weights, channel, place, pump, store):
    inner_weight, gate_weight, out_weight, select_weight, step_weight = weights
    taps, conv_bias, step_bias, decay_log, skip_gain = channel
    normed, inner, gate, conv_out, step_low, raw, sel, mixed, gated, hist = stored
    tokens = normed.shape[0]
    rows = tokens // 8
    flat = lambda v: v.reshape(tokens, -1)
    gated_grad = mm(low_grad, out_weight)
    gated_grad = gated_grad.reshape(gate.shape)
    from_scan = scan_backward(
        conv_out.astype(F32), raw, gate, mixed, gated_grad, hist, sel, step_bias, decay_log, skip_gain, place
    )
    gate_grad, conv_scan, raw_grad, sel_grad, decay_grad, skip_grad, bias_grad = pump.land(tuple(from_scan))

    raw_low = flat(raw_grad).astype(BF)
    step_low_grad = mm_nt(raw_low, step_weight)
    states = [sel_grad[:, :, at].reshape(tokens, -1) for at in (0, ROWS)]
    select_grads = jnp.concatenate([step_low_grad, *states], axis=1)
    gate_low = flat(gate_grad.astype(BF))
    pump.add(settle_job(pump.layout, normed, gate_low, store, "gate"))
    with jax.named_scope("select_return"):
        select_grads = select_grads + exchange(select_grads.astype(BF), "c").astype(F32)
        select_grads = pump.turn(select_grads, 1)
        select_low = chip_total(select_grads).astype(BF)
    select_low = pump.turn(select_low, 0)
    conv_grad = conv_scan + mm(select_low, select_weight).reshape(conv_scan.shape)
    before = conv_total(inner, taps, conv_bias)
    sig = jax.nn.sigmoid(before)
    inner_grad, taps_grad, conv_bias_grad = conv_back(conv_grad * sig * (1.0 + before * (1.0 - sig)), inner, taps)
    inner_low = flat(from_time(inner_grad.astype(BF), rows))
    cut = inner_low.shape[1] // 2
    inner_parts = (inner_low[:, :cut], inner_low[:, cut:])
    for name, part in zip(("inner0", "inner1"), inner_parts):
        pump.add(settle_job(pump.layout, normed, part, store, name))
    small = jnp.concatenate(
        [
            mm_tn(select_low, flat(conv_out)),
            mm_tn(step_low, raw_low),
            taps_grad,
            conv_bias_grad[None],
            jnp.sum(bias_grad, axis=0, keepdims=True),
            decay_grad,
            jnp.sum(skip_grad, axis=0, keepdims=True),
        ],
        axis=0,
    )
    pump.add(small_job(pump.layout, small, store, "small"))
    pump.begin(inner_low, 3)
    return (*zip(inner_parts, inner_weight), (gate_low, gate_weight))


def ffn_backward(stored, low_grad, weights):
    gate_weight, up_weight, down_weight = weights
    normed, gate, up, hidden = stored
    hidden_grad = mm(low_grad, down_weight)
    sig = jax.nn.sigmoid(gate)
    gate_low = (hidden_grad * up * sig * (1.0 + gate * (1.0 - sig))).astype(BF)
    up_low = (hidden_grad * gate * sig).astype(BF)
    return [(gate_low, gate_weight), (up_low, up_weight)]


def shards(
    layout,
    layer_input,
    upstream,
    norm_gains,
    mixer_input,
    conv_taps,
    conv_bias,
    mixer_select,
    mixer_step,
    step_bias,
    decay_log,
    skip_gain,
    mixer_output,
    first_gate_up,
    first_down,
    attention_input,
    attention_output,
    second_gate_up,
    second_down,
):
    mine = lambda v: half_of(v, "b")
    theirs = lambda v: half_of(v, "b", True)
    place = jnp.stack([bit("x"), bit("c")]).astype(jnp.int32)
    quarter = place[0] * 2 + place[1]
    rows = layer_input.shape[0] // QUARTERS
    tokens = 8 * rows
    own_rows = lambda v: layout.columns_in(lax.dynamic_slice_in_dim(v, quarter * rows, rows, axis=0))
    blocks = lambda v: v.reshape(2, 2, 2, rows, v.shape[-1])

    pump, weights, grads = Pump(layout), {}, {}

    def swapped(arrays, *tokens):
        with jax.named_scope("pack"):
            if tokens:
                arrays = lax.optimization_barrier((tuple(arrays),) + tokens)[0]
            flat = lambda v: v.reshape(v.shape[0], -1)
            kept = jnp.concatenate([flat(mine(a)) for a in arrays], axis=1)
            return kept, exchange(jnp.concatenate([flat(theirs(a)) for a in arrays], axis=1), "b")

    def request(names, arrays, *tokens):
        kept, got = swapped(arrays, *tokens)
        width = kept.shape[1] // len(names)
        for at, name in enumerate(names):
            cut = slice(at * width, (at + 1) * width)
            pump.add(fetch_job(layout, kept[:, cut], got[:, cut], weights, name))
        return got

    here, _, wide = attention_input.shape
    width = wide // 2
    stream0 = own_rows(layer_input).astype(F32)
    gains = layout.columns_in(norm_gains)
    upstream_rows = own_rows(upstream)
    with jax.named_scope("inner_fetch"):
        first = request(["inner0", "inner1"], [mixer_input[:, 0]])
        pump.flush()
    normed0 = gather_rows(tied(rms(stream0, gains[0]), first))
    normed_first = normed0
    request(["small"], [jnp.concatenate([mixer_step, mixer_select], axis=0)], normed0)
    pump.flush()
    second = request(["gate", "out"], [mixer_input[:, 1], mixer_output], first)
    third = request(
        ["gate1", "up1", "down1"], [first_gate_up, first_down], normed0, second,
    )
    normed0 = pump.turn(normed0, 1)
    channel = tuple(mine(v) for v in (conv_taps, conv_bias, step_bias, decay_log, skip_gain))
    inner = jnp.concatenate([mm(normed0, weights["inner0"]), mm(normed0, weights["inner1"])], axis=1)
    low4 = gather_rows(tied(upstream_rows, normed_first))
    inner = tied(pump.turn(inner, 1), low4)
    inner = in_time(blocks(inner))
    conv_out = jax.nn.silu(conv_total(inner, channel[0], channel[1])).astype(BF)
    select_rows, step_rows = mixer_select.shape[0], mixer_step.shape[0]
    both = layout.columns_out(weights["small"], 0).reshape(-1, select_rows + step_rows, conv_out.shape[-1])
    select_weight = both[:, step_rows:].reshape(-1, conv_out.shape[-1])
    step_weight = both[:, :step_rows].reshape(-1, conv_out.shape[-1])
    partial = mm_nt(conv_out.reshape(tokens, -1), select_weight)
    with jax.named_scope("select_total"):
        selected = channel_total(partial, True)
    selected = pump.turn(selected)
    request(["query_key", "value_out"], [attention_input, attention_output], inner, third)
    rank, states_n = step_weight.shape[0], decay_log.shape[0]
    step_low = selected[:, :rank].astype(BF)
    raw = mm(step_low, step_weight).reshape(conv_out.shape)
    sel = selected[:, rank:].reshape(2, tokens // 2 // ROWS, ROWS, -1).transpose(0, 1, 3, 2)
    raw = pump.until(raw, weights, "gate")
    gate = blocks(mm(normed0, weights["gate"]))
    mixed, gated, hist = scan_forward(conv_out.astype(F32), raw, gate, sel, *channel[2:], place)
    gated = gated.reshape(tokens, -1).astype(BF)
    gated = pump.until(gated, weights, "out")
    mixer_stored = (normed0, inner, gate, conv_out, step_low, raw, sel, mixed, gated, hist)
    mixer_weights = ((weights["inner0"], weights["inner1"]), weights["gate"], weights["out"], select_weight, step_weight)
    stream1 = pump.turn(stream0 + scatter_rows([(gated, weights["out"])]))
    request(
        ["gate2", "up2", "down2"], [second_gate_up, second_down], gated
    )

    def ffn(normed, tag):
        normed = pump.until(normed, weights, "gate" + tag, "up" + tag)
        gate, up = mm(normed, weights["gate" + tag]), mm(normed, weights["up" + tag])
        hidden = (jax.nn.silu(gate) * up).astype(BF)
        return hidden, (normed, gate, up, hidden)

    hidden1, first_stored = ffn(pump.turn(gather_rows(rms(stream1, gains[1]))), "1")
    hidden1 = pump.until(hidden1, weights, "down1")
    first_weights = tuple(weights[n] for n in ("gate1", "up1", "down1"))
    stream2 = pump.turn(stream1 + scatter_rows([(hidden1, weights["down1"])]))

    normed2 = pump.turn(gather_rows(rms(stream2, gains[2])))
    normed2 = pump.until(normed2, weights, "query_key", "value_out")
    value_weight, out_weight = weights["value_out"][:, :width], weights["value_out"][:, width:]
    triple = jnp.concatenate([mm(normed2, weights["query_key"]), mm(normed2, value_weight)], axis=1)
    order = (jnp.arange(2)[None, :] ^ place[0]) * 2 + (jnp.arange(2)[:, None] ^ place[1])
    tables = rotary_tables((order[:, :, None] * rows + jnp.arange(rows)).reshape(-1))
    turned, context = attention_call(
        attention_forward_kernel, "attention_forward", [blocks(triple)], (3 * width, width), tables
    )
    context = context.reshape(tokens, -1)
    stream3 = pump.turn(stream2 + scatter_rows([(context, out_weight)]))

    hidden3, second_stored = ffn(gather_rows(rms(stream3, gains[3])), "2")
    hidden3 = pump.until(hidden3, weights, "down2")
    second_weights = tuple(weights[n] for n in ("gate2", "up2", "down2"))

    pump.add(settle_job(layout, low4, hidden3, grads, "down2"))
    pump.begin(hidden3, 1)
    products = ffn_backward(second_stored, low4, second_weights)
    normed3 = second_stored[0]
    for name, (right, _) in zip(("gate2", "up2"), products):
        pump.add(settle_job(layout, normed3, right, grads, name))
    back, gain3 = rms_back(stream3, gains[3], pump.turn(scatter_rows(products)))
    grad3 = upstream_rows.astype(F32) + back
    stream4 = stream3 + scatter_rows([(hidden3, weights["down2"])])

    low3 = gather_rows(grad3.astype(BF))
    pump.add(settle_job(layout, low3, context, grads, "attention_out"))
    low3 = pump.turn(low3, 2)
    context_grad = mm(low3, out_weight).astype(BF)
    (triple_low,) = attention_call(
        attention_backward_kernel, "attention_backward", [turned, blocks(context_grad)], (3 * width,), tables
    )
    triple_low = triple_low.reshape(tokens, -1)
    pump.add(settle_job(layout, normed2, triple_low, grads, "attention_in"))
    back, gain2 = rms_back(
        stream2,
        gains[2],
        pump.turn(
            scatter_rows([(triple_low[:, : 2 * width], weights["query_key"]), (triple_low[:, 2 * width :], value_weight)])
        ),
    )
    grad2 = grad3 + back
    low2 = pump.turn(gather_rows(grad2.astype(BF)), 0)
    products = ffn_backward(first_stored, low2, first_weights)
    pump.add(settle_job(layout, low2, first_stored[3], grads, "down1"))
    pump.begin(low2, 1)
    for name, (right, _) in zip(("gate1", "up1"), products):
        pump.add(settle_job(layout, first_stored[0], right, grads, name))
    back, gain1 = rms_back(stream1, gains[1], pump.turn(scatter_rows(products), 2))
    grad1 = grad2 + back

    low1 = gather_rows(grad1.astype(BF))
    pump.add(settle_job(layout, low1, mixer_stored[8], grads, "out"))
    low1 = pump.turn(low1, 1, 1)
    products = mixer_backward(mixer_stored, low1, mixer_weights, channel, place, pump, grads)
    scattered = pump.turn(scatter_rows(products), 0)
    back, gain0 = rms_back(stream0, gains[0], scattered)
    with jax.named_scope("gain_sums"):
        gains_grad = layout.columns_out(jnp.stack([gain0, gain1, gain2, gain3]))
        for axis in ("c", "x", "b") + layout.sums:
            gains_grad = gains_grad + exchange(gains_grad, axis)
    gains_grad = pump.turn(gains_grad, 0)
    pump.flush()
    small = grads["small"]
    with jax.named_scope("last_gather"):
        input_grad = gather_sequence(layout.columns_out((grad1 + back).astype(BF))).astype(F32)
        layer_output = gather_sequence(layout.columns_out(stream4.astype(BF)))

    dp_index = lax.axis_index(layout.high + ("b", "y"))
    select_all, step_all = select_weight.shape[0], step_weight.shape[0]
    select_grad = lax.dynamic_slice_in_dim(small[:select_all], dp_index * select_rows, select_rows, axis=0)
    step_grad = lax.dynamic_slice_in_dim(
        small[select_all : select_all + step_all], dp_index * step_rows, step_rows, axis=0
    )
    rest = small[select_all + step_all :]
    count = conv_taps.shape[0]
    taps_grad, conv_bias_grad, step_bias_grad = rest[:count], rest[count], rest[count + 1]
    decay_grad, skip_grad = rest[count + 2 : count + 2 + states_n], rest[count + 2 + states_n]

    matrix = lambda halves: jnp.concatenate(halves, axis=1).astype(F32)
    pair = lambda low, high: jnp.stack([jnp.concatenate(low, axis=1), jnp.concatenate(high, axis=1)], axis=1).astype(F32)
    parts = lambda halves, count: jnp.stack([h.reshape(here, count, -1) for h in halves], axis=2).astype(F32)
    return (
        layer_output,
        input_grad,
        gains_grad,
        pair([jnp.concatenate(h, axis=1) for h in zip(grads["inner0"], grads["inner1"])], grads["gate"]),
        taps_grad,
        conv_bias_grad,
        select_grad,
        step_grad,
        step_bias_grad,
        decay_grad,
        skip_grad,
        matrix(grads["out"]),
        pair(grads["gate1"], grads["up1"]),
        matrix(grads["down1"]),
        parts(grads["attention_in"], 3).reshape(here, 3, -1),
        matrix(grads["attention_out"]),
        pair(grads["gate2"], grads["up2"]),
        matrix(grads["down2"]),
    )


def solution(mesh):
    n_dp, n_tensor = mesh.devices.shape
    bits = n_dp.bit_length() - 1
    assert n_dp == 1 << bits and bits >= 2 and n_tensor == 4
    high = tuple("a%d" % k for k in range(bits - 2))
    names = high + ("b", "y", "x", "c")
    cube = jax.sharding.Mesh(mesh.devices.reshape((2,) * len(names)), names)
    dp, tensor = high + ("b", "y"), ("x", "c")
    row, both, col = P(dp, None), P(dp, tensor), P(None, tensor)
    three, vec = P(dp, None, tensor), P(tensor)
    return jax.shard_map(
        functools.partial(shards, Layout(high)),
        mesh=cube,
        in_specs=(
            row, row, P(), three, col, vec, both, both, vec, col, vec, both, three, both, three, both, three, both,
        ),
        out_specs=(
            row, row, P(), three, col, vec, both, both, vec, col, vec, both, three, both, three, both, three, both,
        ),
        check_vma=False,
    )
```
